128 devices in a mesh: ctx: 16 (over z_lo, y, core), tp: 4 (over x), fsdp: 2 (over z_hi).
Axes of the slice: x: 4, y: 4, z: 4 (z_hi: 2, z_lo: 2; z = z_hi * 2 + z_lo), core: 2. Of those that a mesh axis runs over, the one named last changes fastest.
Arguments:
- x_input: bfloat16 [2, 4096, 128, 128], P('fsdp', 'ctx', 'tp'), may hold values from -6 to 6
- gate_input: bfloat16 [2, 4096, 128, 128], P('fsdp', 'ctx', 'tp'), may hold values from -6 to 6
- dt_raw: bfloat16 [2, 128, 4096], P('fsdp', 'tp', 'ctx'), may hold values from -4 to 4
- b_input: bfloat16 [2, 4096, 8, 128], P('fsdp', 'ctx', 'tp'), may hold values from -6 to 6
- c_input: bfloat16 [2, 4096, 8, 128], P('fsdp', 'ctx', 'tp'), may hold values from -0.5 to 0.5
- a_log: float32 [128], P('tp'), may hold values from -9 to -3
- dt_bias: float32 [128], P('tp'), may hold values from -1 to 1
- skip_weight: float32 [128], P('tp'), may hold values from 0.5 to 1.5
- norm_gain: float32 [16384], P(('tp', 'fsdp')), may hold values from 0.1 to 1.9
- valid_len: int32 [2], P('fsdp'), may hold values from 2048 to 4096, as said below
- grad_output: bfloat16 [2, 4096, 128, 128], P('fsdp', 'ctx', 'tp'), may hold values from -6 to 6
Outputs:
- grad_x: bfloat16 [2, 4096, 128, 128], P('fsdp', 'ctx', 'tp')
- grad_gate: bfloat16 [2, 4096, 128, 128], P('fsdp', 'ctx', 'tp')
- grad_dt: bfloat16 [2, 128, 4096], P('fsdp', 'tp', 'ctx')
- grad_b: bfloat16 [2, 4096, 8, 128], P('fsdp', 'ctx', 'tp')
- grad_c: bfloat16 [2, 4096, 8, 128], P('fsdp', 'ctx', 'tp')
- grad_a_log: float32 [128], P('tp')
- grad_dt_bias: float32 [128], P('tp')
- grad_skip: float32 [128], P('tp')
- grad_gain: float32 [16384], P(('tp', 'fsdp'))
The draws below stay inside these ranges and needn't reach their ends.
Inputs may be any that keep to these rules, and one draw needn't show every extreme that they name: `valid_len`: the sequences' valid lengths are all different, and the longest is 4096.
All inputs are finite; a program needn't handle non-finite values.
Results may differ from the reference program's by a relative error of at most 0.002.
Values sent between devices are 32-bit elements; how exact they have to be, the bound alone decides.
A program may use at most 192 MiB of HBM per device.

```python
import math
import jax
import jax.numpy as jnp
from jax import lax

HEADS = 128
HEAD_DIM = 128
STATE = 128
GROUPS = 8
SEQ_LEN = 4096
SEQS = 2


def draw_valid_len(key, part):
    key = jax.random.fold_in(key, 11)
    lowest = SEQ_LEN // 2
    choices_count = SEQ_LEN - lowest + 1
    picked = jax.random.permutation(key, choices_count)[:SEQS].astype(jnp.int32) + lowest
    longest = jnp.max(picked)
    return jnp.where(picked == longest, SEQ_LEN, picked).astype(jnp.int32)


def shard_levels(own_key, dims, cuts, low, high):
    level, own = 1.0, jax.random.fold_in(own_key, 6)
    for dim, shards_of in cuts:
        heights = jnp.exp(jax.random.uniform(jax.random.fold_in(own, dim), (shards_of,), jnp.float32, low / len(cuts), high / len(cuts)))
        level = level * jnp.repeat(heights, dims[dim] // shards_of).reshape([-1 if axis == dim else 1 for axis in range(len(dims))])
    return level


def centred(key, dims, deviation, reach, cuts=(), held_as=jnp.bfloat16):
    loudness = shard_levels(key, dims, cuts, -0.22, 0.18) if cuts else 1.0
    entries = jax.random.normal(key, dims, jnp.float32) * deviation * loudness
    return jnp.minimum(jnp.maximum(entries, -reach), reach).astype(held_as)


def setup_inputs(seed: int = 0) -> dict:
    key_list = jax.random.split(jax.random.key(seed), 12)
    return {
        "x_input": centred(key_list[0], (SEQS, SEQ_LEN, HEADS, HEAD_DIM), 1.0, 6.0, ((0, 2), (1, 16), (2, 4))),
        "gate_input": centred(key_list[1], (SEQS, SEQ_LEN, HEADS, HEAD_DIM), 1.0, 6.0, ((0, 2), (1, 16), (2, 4))),
        "dt_raw": centred(key_list[2], (SEQS, HEADS, SEQ_LEN), 1.0, 4.0, ((0, 2), (1, 4), (2, 16))),
        "b_input": centred(key_list[3], (SEQS, SEQ_LEN, GROUPS, STATE), 1.0, 6.0, ((0, 2), (1, 16), (2, 4))),
        "c_input": centred(key_list[4], (SEQS, SEQ_LEN, GROUPS, STATE), STATE ** -0.5, 0.5, ((0, 2), (1, 16), (2, 4))),
        "a_log": jnp.clip(-9.0 + 6.0 * jax.random.uniform(key_list[5], (HEADS,), jnp.float32) ** shard_levels(key_list[5], (HEADS,), ((0, 4),), -0.2, 0.2), -9.0, -3.0),
        "dt_bias": jnp.clip(jax.random.uniform(key_list[6], (HEADS,), jnp.float32, -1.0, 1.0) * shard_levels(key_list[6], (HEADS,), ((0, 4),), -0.4, 0.0), -1.0, 1.0),
        "skip_weight": jnp.clip(0.5 + 1.0 * jax.random.uniform(key_list[7], (HEADS,), jnp.float32) ** shard_levels(key_list[7], (HEADS,), ((0, 4),), -0.2, 0.2), 0.5, 1.5),
        "norm_gain": jnp.clip(1.0 + 0.18 * jax.random.normal(key_list[8], (HEADS * HEAD_DIM,), jnp.float32), 0.1, 1.9),
        "valid_len": draw_valid_len(jax.random.fold_in(key_list[11], 71), 0),
        "grad_output": centred(key_list[10], (SEQS, SEQ_LEN, HEADS, HEAD_DIM), 1.0, 6.0, ((0, 2), (1, 16), (2, 4))),
    }


EPS = 1e-05
HIGH = lax.Precision.HIGHEST

def block_step(decay_rate, carry_state, x_block, step_block, b_block, c_block):
    block_len = step_block.shape[-1]
    running = jnp.cumsum(step_block * decay_rate[..., None], axis=-1)
    log_gaps = running[..., :, None] - running[..., None, :]
    causal = jnp.arange(block_len)[:, None] >= jnp.arange(block_len)[None, :]
    decay_mask = jnp.where(causal, jnp.exp(jnp.where(causal, log_gaps, 0.0)), 0.0)
    scores = jnp.einsum('tgn,sgn->gts', c_block, b_block, precision=HIGH)
    weights = decay_mask * scores[:, None] * step_block[:, :, None, :]
    output = jnp.einsum('gkts,sgkp->tgkp', weights, x_block, precision=HIGH)
    carried = jnp.einsum('tgn,gkpn->tgkp', c_block, carry_state, precision=HIGH)
    output = output + carried * jnp.transpose(jnp.exp(running), (2, 0, 1))[..., None]
    weighting = jnp.exp(running[..., -1:] - running) * step_block
    fresh_state = jnp.einsum('gks,sgkp,sgn->gkpn', weighting, x_block, b_block, precision=HIGH)
    next_state = jnp.exp(running[..., -1])[..., None, None] * carry_state + fresh_state
    return (next_state, output)

def run_blocks(decay_rate, start_state, x_all, step_all, b_all, c_all, block_len):
    length = x_all.shape[0]
    blocks = length // block_len
    x_blocks = x_all.reshape((blocks, block_len) + x_all.shape[1:])
    step_blocks = jnp.moveaxis(step_all.reshape(step_all.shape[:2] + (blocks, block_len)), 2, 0)
    b_blocks = b_all.reshape((blocks, block_len) + b_all.shape[1:])
    c_blocks = c_all.reshape((blocks, block_len) + c_all.shape[1:])

    def advance(carry_state, pieces):
        return block_step(decay_rate, carry_state, pieces[0], pieces[1], pieces[2], pieces[3])
    final_state, outputs = lax.scan(advance, start_state, (x_blocks, step_blocks, b_blocks, c_blocks))
    return outputs.reshape((length,) + outputs.shape[2:])

def mixer_forward(x_all, step_raw, b_all, c_all, gate_all, a_log, dt_bias, skip_weight, norm_gain, start_state, block_len):
    step_size = jax.nn.softplus(step_raw + dt_bias[..., None])
    decay_rate = -jnp.exp(a_log)
    scanned = run_blocks(decay_rate, start_state, x_all, step_size, b_all, c_all, block_len)
    mixed = scanned + skip_weight[None, :, :, None] * x_all
    gated = mixed * jax.nn.silu(gate_all)
    mean_square = lax.optimization_barrier(jnp.mean(gated * gated, axis=(2, 3), keepdims=True))
    return gated * lax.rsqrt(mean_square + EPS) * norm_gain[None]

def reference(x_input, gate_input, dt_raw, b_input, c_input, a_log, dt_bias, skip_weight, norm_gain, valid_len, grad_output):
    per_group = HEADS // GROUPS
    block_len = math.gcd(256, SEQ_LEN)
    position = jnp.arange(SEQ_LEN, dtype=jnp.int32)
    a_groups = a_log.reshape(GROUPS, per_group)
    bias_groups = dt_bias.reshape(GROUPS, per_group)
    skip_groups = skip_weight.reshape(GROUPS, per_group)
    gain_groups = norm_gain.reshape(GROUPS, per_group, HEAD_DIM)
    zero_state = jnp.zeros((1, per_group, HEAD_DIM, STATE), jnp.float32)

    def group_grads(pieces):
        x_grp, gate_grp, step_grp, b_grp, c_grp, a_grp, bias_grp, skip_grp, gain_grp, cot_grp = pieces

        def forward(x_value, gate_value, step_value, b_value, c_value, a_value, bias_value, skip_value, gain_value):
            result = mixer_forward(x_value[:, None], step_value[None], b_value[:, None], c_value[:, None], gate_value[:, None], a_value[None], bias_value[None], skip_value[None], gain_value[None], zero_state, block_len)
            return result[:, 0]
        _, pullback = jax.vjp(forward, x_grp, gate_grp, step_grp, b_grp, c_grp, a_grp, bias_grp, skip_grp, gain_grp)
        return pullback(cot_grp)
    list_x, list_gate, list_step, list_b, list_c = ([], [], [], [], [])
    sum_a = jnp.zeros((HEADS,), jnp.float32)
    sum_bias = jnp.zeros((HEADS,), jnp.float32)
    sum_skip = jnp.zeros((HEADS,), jnp.float32)
    sum_gain = jnp.zeros((HEADS * HEAD_DIM,), jnp.float32)
    for sequence in range(SEQS):
        keep_mask = (position < valid_len[sequence]).astype(jnp.float32)
        x_seq = jnp.moveaxis(x_input[sequence].astype(jnp.float32).reshape(SEQ_LEN, GROUPS, per_group, HEAD_DIM), 1, 0)
        gate_seq = jnp.moveaxis(gate_input[sequence].astype(jnp.float32).reshape(SEQ_LEN, GROUPS, per_group, HEAD_DIM), 1, 0)
        cot_full = grad_output[sequence].astype(jnp.float32) * keep_mask[:, None, None]
        cot_seq = jnp.moveaxis(cot_full.reshape(SEQ_LEN, GROUPS, per_group, HEAD_DIM), 1, 0)
        step_seq = dt_raw[sequence].astype(jnp.float32).reshape(GROUPS, per_group, SEQ_LEN)
        b_seq = jnp.moveaxis(b_input[sequence].astype(jnp.float32), 1, 0)
        c_seq = jnp.moveaxis(c_input[sequence].astype(jnp.float32), 1, 0)
        grads_seq = lax.map(group_grads, (x_seq, gate_seq, step_seq, b_seq, c_seq, a_groups, bias_groups, skip_groups, gain_groups, cot_seq))
        list_x.append(jnp.moveaxis(grads_seq[0], 0, 1).reshape(SEQ_LEN, HEADS, HEAD_DIM))
        list_gate.append(jnp.moveaxis(grads_seq[1], 0, 1).reshape(SEQ_LEN, HEADS, HEAD_DIM))
        list_step.append(grads_seq[2].reshape(HEADS, SEQ_LEN))
        list_b.append(jnp.moveaxis(grads_seq[3], 0, 1))
        list_c.append(jnp.moveaxis(grads_seq[4], 0, 1))
        sum_a = sum_a + grads_seq[5].reshape(HEADS)
        sum_bias = sum_bias + grads_seq[6].reshape(HEADS)
        sum_skip = sum_skip + grads_seq[7].reshape(HEADS)
        sum_gain = sum_gain + grads_seq[8].reshape(HEADS * HEAD_DIM)
    scale = 1.0 / math.sqrt(SEQS * SEQ_LEN)
    return (jnp.stack(list_x).astype(jnp.bfloat16), jnp.stack(list_gate).astype(jnp.bfloat16), jnp.stack(list_step).astype(jnp.bfloat16), jnp.stack(list_b).astype(jnp.bfloat16), jnp.stack(list_c).astype(jnp.bfloat16), sum_a * scale, sum_bias * scale, sum_skip * scale, sum_gain * scale)
```

```python
import functools
import math

import jax
import jax.numpy as jnp
from jax import lax
from jax.experimental import pallas as pl
from jax.experimental.pallas import tpu as pltpu
from jax.sharding import PartitionSpec as P

EPS = 1e-05
HIGH = lax.Precision.HIGHEST
F32 = jnp.float32
BF16 = jnp.bfloat16
MESH = pl.DeviceIdType.MESH
VMEM_LIMIT = 48 * 1024 * 1024


def split(value):
    high = value.astype(BF16)
    return high, (value - high.astype(F32)).astype(BF16)


def dot(left, right):
    return jnp.dot(left, right, preferred_element_type=F32)


def dot_nt(left, right):
    return lax.dot_general(left, right, (((1,), (1,)), ((), ())), preferred_element_type=F32)


def dot_tn(left, right):
    return lax.dot_general(left, right, (((0,), (0,)), ((), ())), preferred_element_type=F32)


def softplus(value):
    return jnp.maximum(value, 0.0) + jnp.log1p(jnp.exp(-jnp.abs(value)))


def sigmoid(value):
    return 1.0 / (1.0 + jnp.exp(-value))


def lower(length):
    row = lax.broadcasted_iota(jnp.int32, (length, length), 0)
    column = lax.broadcasted_iota(jnp.int32, (length, length), 1)
    return row >= column


def local_kernel(x_ref, dt_ref, a_ref, bias_ref, bt_ref, xh_ref, er_ref, es_ref, ec_ref, fresh_ref, wide):
    tokens, heads, dim = x_ref.shape
    wide[...] = x_ref[...].astype(F32).reshape(tokens * heads, dim)
    step = softplus(dt_ref[...].astype(F32) + bias_ref[...])
    log_step = step * (-jnp.exp(a_ref[...]))
    upto = jnp.where(lower(tokens), 1.0, 0.0).astype(F32)
    running = lax.dot_general(
        log_step, upto, (((1,), (1,)), ((), ())), precision=HIGH, preferred_element_type=F32
    )
    half = 0.5 * running[:, tokens - 1 :]
    er_ref[0] = jnp.transpose(jnp.exp(running - half))
    es = jnp.transpose(jnp.exp(half - running) * step)
    es_ref[0] = es
    ec_ref[...] = jnp.broadcast_to(jnp.exp(half), ec_ref.shape)
    for head in range(0, heads, 2):
        scaled = []
        for one in (head, head + 1):
            x_one = wide[pl.ds(one, tokens, stride=heads), :]
            xh_ref[:, one * dim : (one + 1) * dim] = x_one.astype(BF16)
            scaled.append(x_one * es[:, one : one + 1])
        high, low = split(jnp.concatenate(scaled, axis=1))
        state = dot(bt_ref[0], high) + dot(bt_ref[0], low)
        for at, one in enumerate((head, head + 1)):
            fresh_ref[one] = state[:, at * dim : (at + 1) * dim] * ec_ref[one : one + 1, :]


def chain_kernel(
    backward, exchange, fresh_ref, ec_ref, gain_ref, carried_ref, final_ref, gains_ref, send_sem, recv_sem, gain_sem
):
    count = lax.axis_size("ctx")
    me = lax.axis_index("ctx")
    pieces = fresh_ref.shape[0]
    right, left = lax.rem(me + 1, count), lax.rem(me + count - 1, count)
    target = left if backward else right
    place = count - 1 - me if backward else me
    mine = lax.axis_index("fsdp")
    other = 1 - mine
    barrier = pltpu.get_barrier_semaphore()
    for neighbour in (left, right):
        pl.semaphore_signal(barrier, inc=1, device_id={"ctx": neighbour}, device_id_type=MESH)
    if exchange:
        pl.semaphore_signal(barrier, inc=1, device_id={"fsdp": other}, device_id_type=MESH)
    pl.semaphore_wait(barrier, 3 if exchange else 2)

    def piece_copy(at):
        return pltpu.make_async_remote_copy(
            src_ref=final_ref.at[at],
            dst_ref=carried_ref.at[at],
            send_sem=send_sem.at[at],
            recv_sem=recv_sem.at[at],
            device_id={"ctx": target},
            device_id_type=MESH,
        )

    if exchange:
        gains_ref[mine] = gain_ref[...]
        gain_copy = pltpu.make_async_remote_copy(
            src_ref=gain_ref,
            dst_ref=gains_ref.at[mine],
            send_sem=gain_sem.at[0],
            recv_sem=gain_sem.at[1],
            device_id={"fsdp": other},
            device_id_type=MESH,
        )
        gain_copy.start()

    @pl.when(place == 0)
    def _():
        carried_ref[...] = jnp.zeros_like(carried_ref)

    def one(at, carry):
        @pl.when(place > 0)
        def _():
            piece_copy(at).wait_recv()

        decay = ec_ref[pl.ds(at, 1), :]
        final_ref[at] = fresh_ref[at] + (decay * decay) * carried_ref[at]

        @pl.when(place < count - 1)
        def _():
            piece_copy(at).start()

        return carry

    lax.fori_loop(0, pieces, one, 0)

    @pl.when(place < count - 1)
    def _():
        def done(at, carry):
            piece_copy(at).wait_send()
            return carry

        lax.fori_loop(0, pieces, done, 0)

    if exchange:
        gain_copy.wait()


def mixer_kernel(
    limit_ref,
    xh_ref,
    gate_ref,
    out_ref,
    er_ref,
    es_ref,
    ec_ref,
    skip_ref,
    gain_ref,
    state_ref,
    b_ref,
    bt_ref,
    c_ref,
    ct_ref,
    ggate_ref,
    gx_ref,
    local_ref,
    ggain_ref,
    gskip_ref,
    rho_ref,
    sigma_ref,
    gc_ref,
    gb_ref,
    wide_gate,
    wide_out,
    mixed,
):
    tokens, heads, dim = gate_ref.shape
    wide_gate[...] = gate_ref[...].astype(F32).reshape(tokens * heads, dim)
    keep = lax.broadcasted_iota(jnp.int32, (tokens, 1, 1), 0) < limit_ref[0]
    wide_out[...] = jnp.where(keep, out_ref[...].astype(F32), 0.0).reshape(tokens * heads, dim)
    er, es = er_ref[0], es_ref[0]
    causal = lower(tokens)
    scores = jnp.where(causal, dot(c_ref[0], bt_ref[0]), 0.0)
    m_high, m_low = split(scores)
    scores_t = jnp.transpose(scores)
    mt_high, mt_low = split(scores_t)

    def scaled_pair(head):
        return jnp.concatenate(
            [
                xh_ref[:, one * dim : (one + 1) * dim].astype(F32) * es[:, one : one + 1]
                for one in (head, head + 1)
            ],
            axis=1,
        )

    def state_pair(head):
        return jnp.concatenate(
            [state_ref[one] * ec_ref[one : one + 1, :] for one in (head, head + 1)], axis=1
        )

    square = jnp.zeros((tokens, dim), F32)
    cross = jnp.zeros((tokens, dim), F32)
    for head in range(0, heads, 2):
        x_high, x_low = split(scaled_pair(head))
        s_high, s_low = split(state_pair(head))
        scanned = dot(m_high, x_high) + dot(m_high, x_low) + dot(m_low, x_high)
        scanned = scanned + dot(c_ref[0], s_high) + dot(c_ref[0], s_low)
        for at, one in enumerate((head, head + 1)):
            x_one = xh_ref[:, one * dim : (one + 1) * dim].astype(F32)
            mix = scanned[:, at * dim : (at + 1) * dim] * er[:, one : one + 1]
            mix = mix + x_one * skip_ref[one : one + 1, :]
            mixed[:, one * dim : (one + 1) * dim] = mix
            gate = wide_gate[pl.ds(one, tokens, stride=heads), :]
            gated = mix * gate * sigmoid(gate)
            upper = wide_out[pl.ds(one, tokens, stride=heads), :] * gain_ref[one : one + 1, :]
            square = square + gated * gated
            cross = cross + upper * gated
    width = heads * dim
    inverse = lax.rsqrt(jnp.sum(square, axis=1, keepdims=True) * (1.0 / width) + EPS)
    pull = inverse * inverse * inverse * (jnp.sum(cross, axis=1, keepdims=True) * (1.0 / width))
    lane = lax.broadcasted_iota(jnp.int32, (tokens, heads), 1)
    rho = jnp.zeros((tokens, heads), F32)
    sigma = jnp.zeros((tokens, heads), F32)
    grad_m = jnp.zeros((tokens, tokens), F32)
    grad_c = jnp.zeros((tokens, dim), F32)
    for head in range(0, heads, 2):
        scaled, grads = [], []
        for one in (head, head + 1):
            gate = wide_gate[pl.ds(one, tokens, stride=heads), :]
            sig = sigmoid(gate)
            silu = gate * sig
            mix = mixed[:, one * dim : (one + 1) * dim]
            gated = mix * silu
            cot = wide_out[pl.ds(one, tokens, stride=heads), :]
            gain_row = gain_ref[one : one + 1, :]
            ggain_ref[one : one + 1, :] = jnp.sum(cot * gated * inverse, axis=0, keepdims=True)
            grad_gated = inverse * (cot * gain_row) - pull * gated
            grad_mix = grad_gated * silu
            wide_gate[pl.ds(one, tokens, stride=heads), :] = (
                grad_gated * mix * (sig + silu * (1.0 - sig))
            )
            x_one = xh_ref[:, one * dim : (one + 1) * dim].astype(F32)
            skip_x = x_one * skip_ref[one : one + 1, :]
            gskip_ref[one : one + 1, :] = jnp.sum(grad_mix * x_one, axis=0, keepdims=True)
            gx_ref[:, one * dim : (one + 1) * dim] = grad_mix * skip_ref[one : one + 1, :]
            rho = jnp.where(
                lane == one, jnp.sum(grad_mix * (mix - skip_x), axis=1, keepdims=True), rho
            )
            grads.append(grad_mix * er[:, one : one + 1])
        y_high, y_low = split(jnp.concatenate(grads, axis=1))
        back = dot(ct_ref[0], y_high) + dot(ct_ref[0], y_low)
        x_high, x_low = split(scaled_pair(head))
        s_high, s_low = split(state_pair(head))
        grad_m = grad_m + dot_nt(y_high, x_high) + dot_nt(y_high, x_low) + dot_nt(y_low, x_high)
        grad_c = grad_c + dot_nt(y_high, s_high) + dot_nt(y_high, s_low) + dot_nt(y_low, s_high)
        grad_scaled = dot(mt_high, y_high) + dot(mt_high, y_low) + dot(mt_low, y_high)
        for at, one in enumerate((head, head + 1)):
            local_ref[one] = back[:, at * dim : (at + 1) * dim] * ec_ref[one : one + 1, :]
            inner = grad_scaled[:, at * dim : (at + 1) * dim] * es[:, one : one + 1]
            x_one = xh_ref[:, one * dim : (one + 1) * dim].astype(F32)
            sigma = jnp.where(lane == one, jnp.sum(inner * x_one, axis=1, keepdims=True), sigma)
            gx_ref[:, one * dim : (one + 1) * dim] += inner
    ggate_ref[...] = wide_gate[...].reshape(tokens, heads, dim).astype(BF16)
    rho_ref[0] = rho
    sigma_ref[0] = sigma
    grad_m = jnp.where(causal, grad_m, 0.0)
    g_high, g_low = split(grad_m)
    gc_ref[0] = (grad_c + dot(g_high, b_ref[0]) + dot(g_low, b_ref[0])).astype(BF16)
    t_high, t_low = split(jnp.transpose(grad_m))
    gb_ref[0] = dot(t_high, c_ref[0]) + dot(t_low, c_ref[0])


def final_kernel(
    xh_ref,
    es_ref,
    ec_ref,
    behind_ref,
    end_ref,
    b_ref,
    gx_ref,
    gb_ref,
    rho_ref,
    sigma_ref,
    gskip_ref,
    dt_ref,
    a_ref,
    bias_ref,
    gx_out,
    gb_out,
    gdt_out,
    small_out,
    wide,
    rows,
):
    tokens, heads, dim = gx_out.shape
    es = es_ref[0]
    lane = lax.broadcasted_iota(jnp.int32, (tokens, heads), 1)
    sigma = jnp.zeros((tokens, heads), F32)
    grad_b = gb_ref[0]
    for head in range(0, heads, 2):
        scaled, states = [], []
        for one in (head, head + 1):
            scaled.append(
                xh_ref[:, one * dim : (one + 1) * dim].astype(F32) * es[:, one : one + 1]
            )
            states.append(behind_ref[one] * ec_ref[one : one + 1, :])
            rows[one : one + 1, :] = jnp.sum(behind_ref[one] * end_ref[one], axis=0, keepdims=True)
        x_high, x_low = split(jnp.concatenate(scaled, axis=1))
        s_high, s_low = split(jnp.concatenate(states, axis=1))
        grad_b = grad_b + dot_nt(x_high, s_high) + dot_nt(x_high, s_low) + dot_nt(x_low, s_high)
        grad_scaled = dot(b_ref[0], s_high) + dot(b_ref[0], s_low)
        for at, one in enumerate((head, head + 1)):
            inner = grad_scaled[:, at * dim : (at + 1) * dim] * es[:, one : one + 1]
            x_one = xh_ref[:, one * dim : (one + 1) * dim].astype(F32)
            sigma = jnp.where(lane == one, jnp.sum(inner * x_one, axis=1, keepdims=True), sigma)
            wide[pl.ds(one, tokens, stride=heads), :] = (
                gx_ref[:, one * dim : (one + 1) * dim] + inner
            )
    gx_out[...] = wide[...].reshape(tokens, heads, dim).astype(BF16)
    gb_out[0] = grad_b.astype(BF16)
    sigma = sigma + sigma_ref[0]
    after = jnp.where(lower(tokens), 1.0, 0.0).astype(F32)
    sums = lax.dot_general(
        rho_ref[0] - sigma, after, (((0,), (0,)), ((), ())), precision=HIGH, preferred_element_type=F32
    )
    sigma_t = jnp.transpose(sigma)
    grad_log = sums + jnp.sum(rows[...], axis=1, keepdims=True)
    value = dt_ref[...].astype(F32) + bias_ref[...]
    step = softplus(value)
    rate = -jnp.exp(a_ref[...])
    grad_dt = (sigma_t / step + grad_log * rate) * sigmoid(value)
    gdt_out[...] = grad_dt.astype(BF16)
    grad_a = jnp.sum(grad_log * step, axis=1, keepdims=True) * rate
    grad_bias = jnp.sum(grad_dt, axis=1, keepdims=True)
    grad_skip = jnp.sum(gskip_ref[...], axis=1, keepdims=True)
    place = lax.broadcasted_iota(jnp.int32, small_out.shape, 1)
    small_out[...] = jnp.where(
        place == 0, grad_a, jnp.where(place == 1, grad_bias, jnp.where(place == 2, grad_skip, 0.0))
    )


def reduce_kernel(
    scale, gain_ref, small_ref, gain_out, small_out, first, gathered, first_sem, send_sem, recv_sem
):
    count = lax.axis_size("ctx")
    me = lax.axis_index("ctx")
    mine = lax.axis_index("fsdp")
    other = 1 - mine
    half = gain_out.shape[0]
    barrier = pltpu.get_barrier_semaphore()
    pl.semaphore_signal(barrier, inc=1, device_id={"fsdp": other}, device_id_type=MESH)
    for hop in range(1, count):
        pl.semaphore_signal(
            barrier, inc=1, device_id={"ctx": lax.rem(me + hop, count)}, device_id_type=MESH
        )
    pl.semaphore_wait(barrier, count)
    first[0, :half] = gain_ref[pl.ds(pl.multiple_of(other * half, half), half), :]
    first[0, half:] = small_ref[...]
    swap = pltpu.make_async_remote_copy(
        src_ref=first.at[0],
        dst_ref=first.at[1],
        send_sem=first_sem.at[0],
        recv_sem=first_sem.at[1],
        device_id={"fsdp": other},
        device_id_type=MESH,
    )
    swap.start()
    swap.wait()
    gathered[0, :half] = first[1, :half] + gain_ref[pl.ds(pl.multiple_of(mine * half, half), half), :]
    gathered[0, half:] = first[1, half:] + small_ref[...]

    def piece_copy(hop):
        return pltpu.make_async_remote_copy(
            src_ref=gathered.at[0],
            dst_ref=gathered.at[hop],
            send_sem=send_sem.at[hop],
            recv_sem=recv_sem.at[hop],
            device_id={"ctx": lax.rem(me + hop, count)},
            device_id_type=MESH,
        )

    for hop in range(1, count):
        piece_copy(hop).start()
    for hop in range(1, count):
        piece_copy(hop).wait()
    total = gathered[0]
    for hop in range(1, count):
        total = total + gathered[hop]
    gain_out[...] = total[:half] * scale
    small_out[...] = total[half:] * scale


def per_device(
    x_input,
    gate_input,
    dt_raw,
    b_input,
    c_input,
    a_log,
    dt_bias,
    skip_weight,
    norm_gain,
    valid_len,
    grad_output,
):
    _, tokens, heads, dim = x_input.shape
    groups, state = b_input.shape[2:]
    per_group = heads // groups
    count = lax.axis_size("ctx")
    width = per_group * dim
    shape = jax.ShapeDtypeStruct
    whole = pl.BlockSpec(memory_space=pltpu.VMEM)

    def params(**extra):
        return pltpu.CompilerParams(vmem_limit_bytes=VMEM_LIMIT, **extra)

    natural = pl.BlockSpec((tokens, per_group, dim), lambda g: (0, g, 0))
    flat = pl.BlockSpec((tokens, width), lambda g: (0, g))
    times = pl.BlockSpec((per_group, tokens), lambda g: (g, 0))
    column = pl.BlockSpec((per_group, 1), lambda g: (g, 0))
    line = pl.BlockSpec((per_group, dim), lambda g: (g, 0))
    states = pl.BlockSpec((per_group, state, dim), lambda g: (g, 0, 0))
    token_head = pl.BlockSpec((1, tokens, per_group), lambda g: (g, 0, 0))
    tall = pl.BlockSpec((1, tokens, state), lambda g: (g, 0, 0))
    broad = pl.BlockSpec((1, state, tokens), lambda g: (g, 0, 0))

    b_tall = jnp.transpose(b_input[0], (1, 0, 2))
    c_tall = jnp.transpose(c_input[0], (1, 0, 2))
    b_broad = jnp.transpose(b_input[0], (1, 2, 0))
    c_broad = jnp.transpose(c_input[0], (1, 2, 0))
    a_column = a_log[:, None]
    bias_column = dt_bias[:, None]
    skip_line = jnp.broadcast_to(skip_weight[:, None], (heads, dim))
    limit = valid_len - lax.axis_index("ctx") * tokens

    xh, er, es, ec, fresh = pl.pallas_call(
        local_kernel,
        grid=(groups,),
        in_specs=[natural, times, column, column, broad],
        out_specs=[flat, token_head, token_head, line, states],
        out_shape=[
            shape((tokens, heads * dim), BF16),
            shape((groups, tokens, per_group), F32),
            shape((groups, tokens, per_group), F32),
            shape((heads, dim), F32),
            shape((heads, state, dim), F32),
        ],
        scratch_shapes=[pltpu.VMEM((tokens * per_group, dim), F32)],
        compiler_params=params(),
        name="local_states",
    )(x_input[0], dt_raw[0], a_column, bias_column, b_broad)

    def chain(backward, fresh_states, gain):
        return pl.pallas_call(
            functools.partial(chain_kernel, backward, not backward),
            in_specs=[whole] * 3,
            out_specs=[whole] * 3,
            out_shape=[
                shape((heads, state, dim), F32),
                shape((heads, state, dim), F32),
                shape((2, heads // 2, dim), F32),
            ],
            scratch_shapes=[
                pltpu.SemaphoreType.DMA((heads,)),
                pltpu.SemaphoreType.DMA((heads,)),
                pltpu.SemaphoreType.DMA((2,)),
            ],
            compiler_params=params(collective_id=1 if backward else 0, has_side_effects=True),
            name="chain_backward" if backward else "chain_forward",
        )(fresh_states, ec, gain)

    own_gain = norm_gain.reshape(heads // 2, dim)
    carried, ends, gains = chain(False, fresh, own_gain)

    ggate, gx_part, local, ggain, gskip, rho, sigma, grad_c, gb_part = pl.pallas_call(
        mixer_kernel,
        grid=(groups,),
        in_specs=[
            pl.BlockSpec(memory_space=pltpu.SMEM),
            flat,
            natural,
            natural,
            token_head,
            token_head,
            line,
            line,
            line,
            states,
            tall,
            broad,
            tall,
            broad,
        ],
        out_specs=[natural, flat, states, line, line, token_head, token_head, tall, tall],
        out_shape=[
            shape((tokens, heads, dim), BF16),
            shape((tokens, heads * dim), F32),
            shape((heads, state, dim), F32),
            shape((heads, dim), F32),
            shape((heads, dim), F32),
            shape((groups, tokens, per_group), F32),
            shape((groups, tokens, per_group), F32),
            shape((groups, tokens, state), BF16),
            shape((groups, tokens, state), F32),
        ],
        scratch_shapes=[
            pltpu.VMEM((tokens * per_group, dim), F32),
            pltpu.VMEM((tokens * per_group, dim), F32),
            pltpu.VMEM((tokens, width), F32),
        ],
        compiler_params=params(),
        name="mixer",
    )(
        limit,
        xh,
        gate_input[0],
        grad_output[0],
        er,
        es,
        ec,
        skip_line,
        gains.reshape(heads, dim),
        carried,
        b_tall,
        b_broad,
        c_tall,
        c_broad,
    )

    behind, _, _ = chain(True, local, own_gain)

    grad_x, grad_b, grad_dt, small = pl.pallas_call(
        final_kernel,
        grid=(groups,),
        in_specs=[
            flat,
            token_head,
            line,
            states,
            states,
            tall,
            flat,
            tall,
            token_head,
            token_head,
            line,
            times,
            column,
            column,
        ],
        out_specs=[natural, tall, times, line],
        out_shape=[
            shape((tokens, heads, dim), BF16),
            shape((groups, tokens, state), BF16),
            shape((heads, tokens), BF16),
            shape((heads, dim), F32),
        ],
        scratch_shapes=[
            pltpu.VMEM((tokens * per_group, dim), F32),
            pltpu.VMEM((per_group, dim), F32),
        ],
        compiler_params=params(),
        name="final",
    )(
        xh,
        es,
        ec,
        behind,
        ends,
        b_tall,
        gx_part,
        gb_part,
        rho,
        sigma,
        gskip,
        dt_raw[0],
        a_column,
        bias_column,
    )

    scale = 1.0 / math.sqrt(tokens * count * lax.axis_size("fsdp"))
    rows = heads // 2 + heads
    gain_total, small_total = pl.pallas_call(
        functools.partial(reduce_kernel, scale),
        in_specs=[whole] * 2,
        out_specs=[whole] * 2,
        out_shape=[shape((heads // 2, dim), F32), shape((heads, dim), F32)],
        scratch_shapes=[
            pltpu.VMEM((2, rows, dim), F32),
            pltpu.VMEM((count, rows, dim), F32),
            pltpu.SemaphoreType.DMA((2,)),
            pltpu.SemaphoreType.DMA((count,)),
            pltpu.SemaphoreType.DMA((count,)),
        ],
        compiler_params=params(collective_id=2, has_side_effects=True),
        name="reduce_small",
    )(ggain, small)

    return (
        grad_x[None],
        ggate[None],
        grad_dt[None],
        jnp.transpose(grad_b, (1, 0, 2))[None],
        jnp.transpose(grad_c, (1, 0, 2))[None],
        small_total[:, 0],
        small_total[:, 1],
        small_total[:, 2],
        gain_total.reshape(heads // 2 * dim),
    )


def solution(mesh):
    placed = (
        P("fsdp", "ctx", "tp", None),
        P("fsdp", "ctx", "tp", None),
        P("fsdp", "tp", "ctx"),
        P("fsdp", "ctx", "tp", None),
        P("fsdp", "ctx", "tp", None),
        P("tp"),
        P("tp"),
        P("tp"),
        P(("tp", "fsdp")),
        P("fsdp"),
        P("fsdp", "ctx", "tp", None),
    )
    return jax.shard_map(
        per_device,
        mesh=mesh,
        in_specs=placed,
        out_specs=(
            P("fsdp", "ctx", "tp", None),
            P("fsdp", "ctx", "tp", None),
            P("fsdp", "tp", "ctx"),
            P("fsdp", "ctx", "tp", None),
            P("fsdp", "ctx", "tp", None),
            P("tp"),
            P("tp"),
            P("tp"),
            P(("tp", "fsdp")),
        ),
        check_vma=False,
    )
```

```python
import functools
import math

import jax
import jax.numpy as jnp
from jax import lax
from jax.experimental import pallas as pl
from jax.experimental.pallas import tpu as pltpu
from jax.sharding import PartitionSpec as P

EPS = 1e-05
HIGH = lax.Precision.HIGHEST
F32 = jnp.float32
BF16 = jnp.bfloat16
MESH = pl.DeviceIdType.MESH
VMEM_LIMIT = 60 * 1024 * 1024
RING, CORES = 4, 2


def split(value):
    high = value.astype(BF16)
    return high, (value - high.astype(F32)).astype(BF16)


def dot(left, right):
    return jnp.dot(left, right, preferred_element_type=F32)


def dot_nt(left, right):
    return lax.dot_general(left, right, (((1,), (1,)), ((), ())), preferred_element_type=F32)


def softplus(value):
    return jnp.maximum(value, 0.0) + jnp.log1p(jnp.exp(-jnp.abs(value)))


def sigmoid(value):
    return 1.0 / (1.0 + jnp.exp(-value))


def lower(length):
    row = lax.broadcasted_iota(jnp.int32, (length, length), 0)
    column = lax.broadcasted_iota(jnp.int32, (length, length), 1)
    return row >= column


def loop(count, body):
    def one(at, carry):
        body(at)
        return carry

    lax.fori_loop(0, count, one, 0)


def wide(parts):
    return jnp.concatenate(parts, axis=1)


def tall(parts):
    return jnp.concatenate(parts, axis=0)


def mixer_kernel(
    scale,
    groups,
    limit_ref,
    x_hbm,
    gate_hbm,
    out_hbm,
    dt_ref,
    b_ref,
    c_ref,
    a_ref,
    bias_ref,
    skip_ref,
    gain_ref,
    gx_hbm,
    ggate_hbm,
    gdt_ref,
    gb_ref,
    gc_ref,
    small_out,
    gain_out,
    x_in,
    gate_in,
    out_in,
    xh,
    xs_high,
    xs_low,
    esb,
    erb,
    cots,
    silus,
    slopes,
    mixed,
    y_high,
    y_low,
    fresh,
    carried,
    local,
    behind,
    sib,
    pair,
    scat,
    pref,
    ret,
    total,
    ztotal,
    causal_m,
    causal_t,
    bt,
    bb,
    cc,
    ctct,
    ec_ref,
    decays,
    gains,
    skip_line,
    row_ref,
    rho_ref,
    sigma_ref,
    square,
    cross,
    grad_m,
    grad_c,
    grad_b,
    halves,
    ggain,
    gskip,
    rows,
    gain_swap,
    gain_all,
    small_swap,
    small_all,
    in_sem,
    out_sem,
    decay_send,
    decay_recv,
    send_sem,
    recv_sem,
    gain_send,
    gain_recv,
    small_send,
    small_recv,
):
    tokens, heads, dim = x_in.shape
    per = heads // groups
    half = per // CORES
    own = half // RING
    count = lax.axis_size("ctx")
    me = lax.axis_index("ctx")
    ring_len = RING * CORES
    z = me // ring_len
    q = lax.rem(me, ring_len)
    y = q // CORES
    c = lax.rem(q, CORES)
    mine = lax.axis_index("fsdp")
    other = 1 - mine

    def copy_in(at):
        source, target = ((x_hbm, x_in), (gate_hbm, gate_in), (out_hbm, out_in))[at]
        return pltpu.make_async_copy(source, target, in_sem.at[at])

    for at in range(3):
        copy_in(at).start()
    barrier = pltpu.get_barrier_semaphore()
    pl.semaphore_signal(barrier, inc=1, device_id={"fsdp": other}, device_id_type=MESH)
    for hop in range(1, count):
        pl.semaphore_signal(
            barrier, inc=1, device_id={"ctx": lax.rem(me + hop, count)}, device_id_type=MESH
        )

    diagonal = lax.broadcasted_iota(jnp.int32, (heads, heads), 0) == lax.broadcasted_iota(
        jnp.int32, (heads, heads), 1
    )

    def column(ref):
        return jnp.sum(jnp.where(diagonal, ref[...], 0.0), axis=1, keepdims=True)

    rate = -jnp.exp(column(a_ref))
    bias = column(bias_ref)
    skip_line[...] = jnp.broadcast_to(column(skip_ref), skip_line.shape)
    step = softplus(dt_ref[...].astype(F32) + bias)
    ones = jnp.where(lower(tokens), 1.0, 0.0).astype(F32)
    running = lax.dot_general(
        step * rate, ones, (((1,), (1,)), ((), ())), precision=HIGH, preferred_element_type=F32
    )
    middle = 0.5 * running[:, tokens - 1 :]
    er = jnp.transpose(jnp.exp(running - middle))
    es = jnp.transpose(jnp.exp(middle - running) * step)
    ec = jnp.exp(middle)
    ec_ref[...] = jnp.broadcast_to(ec, ec_ref.shape)
    decays[q] = jnp.broadcast_to(ec * ec, ec_ref.shape)

    pl.semaphore_wait(barrier, count)

    def decay_copy(hop):
        return pltpu.make_async_remote_copy(
            src_ref=decays.at[q],
            dst_ref=decays.at[q],
            send_sem=decay_send.at[hop],
            recv_sem=decay_recv.at[hop],
            device_id={"ctx": z * ring_len + lax.rem(q + hop, ring_len)},
            device_id_type=MESH,
        )

    for hop in range(1, ring_len):
        decay_copy(hop).start()

    def gain_copy():
        return pltpu.make_async_remote_copy(
            src_ref=gain_ref,
            dst_ref=gains.at[mine],
            send_sem=gain_send.at[0],
            recv_sem=gain_recv.at[0],
            device_id={"fsdp": other},
            device_id_type=MESH,
        )

    gain_copy().start()
    gains[mine] = gain_ref[...]

    halves[...] = b_ref[...].astype(F32)
    b_groups = [halves[pl.ds(g, tokens, stride=groups), :] for g in range(groups)]
    halves[...] = c_ref[...].astype(F32)
    c_groups = [halves[pl.ds(g, tokens, stride=groups), :] for g in range(groups)]
    for g in range(groups):
        b_one, c_one = b_groups[g].astype(BF16), c_groups[g].astype(BF16)
        b_turn = jnp.transpose(b_groups[g]).astype(BF16)
        c_turn = jnp.transpose(c_groups[g]).astype(BF16)
        bt[g] = wide([b_turn, b_turn])
        bb[g] = wide([b_one, b_one])
        cc[g] = wide([c_one, c_one])
        ctct[g] = wide([c_turn, c_turn])

    def remote(later, g, which, source, target, device):
        at = (int(later) * groups + g) * 9 + which
        return pltpu.make_async_remote_copy(
            src_ref=source,
            dst_ref=target,
            send_sem=send_sem.at[at],
            recv_sem=recv_sem.at[at],
            device_id={"ctx": device},
            device_id_type=MESH,
        )

    sibling = z * ring_len + y * CORES + (1 - c)

    def ring_device(hop):
        return z * ring_len + lax.rem(y + hop, RING) * CORES + c

    def first_swap(later, g):
        source = local if later else fresh
        return remote(
            later,
            g,
            0,
            source.at[pl.ds(g * per + (1 - c) * half, half)],
            sib.at[pl.ds(g * half, half)],
            sibling,
        )

    def scatter(later, g, hop):
        to = lax.rem(y + hop, RING)
        return remote(
            later,
            g,
            hop,
            pair.at[pl.ds(g * half + to * own, own)],
            scat.at[pl.ds(g * half + y * own, own)],
            ring_device(hop),
        )

    def cross_z(later, g):
        return remote(
            later,
            g,
            7,
            total.at[pl.ds(g * own, own)],
            ztotal.at[pl.ds(g * own, own)],
            (1 - z) * ring_len + q,
        )

    def give_back(later, g, hop):
        to = lax.rem(y + hop, RING)
        return remote(
            later,
            g,
            3 + hop,
            pref.at[pl.ds(g * half + to * own, own)],
            ret.at[pl.ds(g * half + y * own, own)],
            ring_device(hop),
        )

    def second_swap(later, g):
        target = behind if later else carried
        return remote(
            later,
            g,
            8,
            ret.at[pl.ds(g * half, half)],
            target.at[pl.ds(g * per + c * half, half)],
            sibling,
        )

    def combine(later, g):
        source = local if later else fresh
        second = 0 if later else 1
        first_swap(later, g).wait()

        def one(k):
            head = g * per + c * half + k
            decay = decays[y * CORES + second, pl.ds(head, 1), :]
            is_second = c == second
            mul_own = jnp.where(is_second, 1.0, decay)
            mul_sib = jnp.where(is_second, decay, 1.0)
            value = source[head] * mul_own + sib[g * half + k] * mul_sib
            pair[g * half + k] = value

        loop(half, one)
        for hop in range(1, RING):
            scatter(later, g, hop).start()
        for j in range(own):
            scat[g * half + y * own + j] = pair[g * half + y * own + j]

    def prefixes(later, g):
        for hop in range(1, RING):
            scatter(later, g, hop).wait()
        order = list(range(RING))[:: -1 if later else 1]
        for j in range(own):
            head = g * per + c * half + y * own + j
            state = jnp.zeros_like(scat[0])
            for chip in order:
                decay = decays[chip * CORES, pl.ds(head, 1), :] * decays[chip * CORES + 1, pl.ds(head, 1), :]
                pref[g * half + chip * own + j] = state
                state = scat[g * half + chip * own + j] + decay * state
            total[g * own + j] = state

        @pl.when(z == (1 if later else 0))
        def _():
            cross_z(later, g).start()
            for hop in range(1, RING):
                give_back(later, g, hop).start()

    def second_chips(later, g):
        @pl.when(z == (0 if later else 1))
        def _():
            cross_z(later, g).wait_recv()
            order = list(range(RING))[:: -1 if later else 1]
            for j in range(own):
                head = g * per + c * half + y * own + j
                state = ztotal[g * own + j]
                for chip in order:
                    decay = decays[chip * CORES, pl.ds(head, 1), :] * decays[chip * CORES + 1, pl.ds(head, 1), :]
                    pref[g * half + chip * own + j] += state
                    state = decay * state
            for hop in range(1, RING):
                give_back(later, g, hop).start()

    def returned(later, g):
        source = local if later else fresh
        target = behind if later else carried
        first = 1 if later else 0
        for j in range(own):
            ret[g * half + y * own + j] = pref[g * half + y * own + j]
        for hop in range(1, RING):
            give_back(later, g, hop).wait()

        @pl.when(z == (1 if later else 0))
        def _():
            cross_z(later, g).wait_send()

        def one(k):
            head = g * per + c * half + k
            decay = decays[y * CORES + first, pl.ds(head, 1), :]
            is_first = c == first
            before = ret[g * half + k]
            base = jnp.where(is_first, source[head], sib[g * half + k])
            after = base + decay * before
            target[head] = jnp.where(is_first, before, after)
            ret[g * half + k] = jnp.where(is_first, after, before)

        loop(half, one)
        second_swap(later, g).start()

    def states(g):
        temp = cots.at[g]
        temp[...] = x_in[:, g * per : (g + 1) * per, :].astype(F32).reshape(tokens * per, dim)
        for one in range(per):
            esb[g * per + one] = jnp.broadcast_to(
                es[:, g * per + one : g * per + one + 1], (tokens, dim)
            )

        def pair_at(hh):
            scaled = []
            for at in range(2):
                head = g * per + hh + at
                x_one = temp[pl.ds(hh + at, tokens, stride=per), :]
                xh[head] = x_one.astype(BF16)
                high, low = split(x_one * esb[head])
                xs_high[head] = high
                xs_low[head] = low
                scaled.append(tall([high, low]))
            state = dot(bt[g], wide(scaled))
            for at in range(2):
                head = g * per + hh + at
                fresh[head] = state[:, at * dim : (at + 1) * dim] * ec_ref[pl.ds(head, 1), :]

        loop(half // 2, lambda i: pair_at((1 - c) * half + 2 * i))
        first_swap(False, g).start()
        loop(half // 2, lambda i: pair_at(c * half + 2 * i))

    def scores(g):
        value = jnp.where(lower(tokens), dot(cc[g, :, :dim], bt[g, :, :tokens]), 0.0)
        high, low = split(value)
        causal_m[g] = wide([high, high, low])
        high, low = split(jnp.transpose(value))
        causal_t[g] = wide([high, high, low])

    def widen(g):
        temp = cots.at[g]
        temp[...] = gate_in[:, g * per : (g + 1) * per, :].astype(F32).reshape(tokens * per, dim)

        def one(hh):
            gate = temp[pl.ds(hh, tokens, stride=per), :]
            sig = sigmoid(gate)
            silu = gate * sig
            place = pl.ds(pl.multiple_of(hh * tokens, tokens), tokens)
            silus[g, place, :] = silu
            slopes[g, place, :] = sig + silu * (1.0 - sig)

        loop(per, one)
        keep = lax.broadcasted_iota(jnp.int32, (tokens, 1, 1), 0) < limit_ref[0]
        temp[...] = jnp.where(
            keep, out_in[:, g * per : (g + 1) * per, :].astype(F32), 0.0
        ).reshape(tokens * per, dim)

    def inside(g):
        for one in range(per):
            erb[g * per + one] = jnp.broadcast_to(
                er[:, g * per + one : g * per + one + 1], (tokens, dim)
            )

        def pair_at(i):
            hh = g * per + 2 * i
            right = wide(
                [tall([xs_high[hh + at], xs_low[hh + at], xs_high[hh + at]]) for at in range(2)]
            )
            scanned = dot(causal_m[g], right)
            for at in range(2):
                head = hh + at
                mixed[head] = scanned[:, at * dim : (at + 1) * dim] * erb[head] + xh[head].astype(
                    F32
                ) * skip_line[pl.ds(head, 1), :]

        loop(per // 2, pair_at)

    def gated_norm(g):
        square[...] = jnp.zeros_like(square)
        cross[...] = jnp.zeros_like(cross)

        def pair_at(i):
            hh = 2 * i
            right = []
            for at in range(2):
                head = g * per + hh + at
                right.append(tall(split(carried[head] * ec_ref[pl.ds(head, 1), :])))
            scanned = dot(cc[g], wide(right))
            sum_square, sum_cross = square[...], cross[...]
            for at in range(2):
                head = g * per + hh + at
                mix = mixed[head] + scanned[:, at * dim : (at + 1) * dim] * erb[head]
                mixed[head] = mix
                place = pl.ds(pl.multiple_of((hh + at) * tokens, tokens), tokens)
                gated = mix * silus[g, place, :]
                cot = cots[g, pl.ds(hh + at, tokens, stride=per), :]
                upper = cot * gains[g, pl.ds(hh + at, 1), :]
                sum_square = sum_square + gated * gated
                sum_cross = sum_cross + upper * gated
            square[...] = sum_square
            cross[...] = sum_cross

        loop(per // 2, pair_at)
        width = per * dim
        inverse = lax.rsqrt(jnp.sum(square[...], axis=1, keepdims=True) * (1.0 / width) + EPS)
        pull = inverse * inverse * inverse * (jnp.sum(cross[...], axis=1, keepdims=True) * (1.0 / width))
        square[...] = jnp.broadcast_to(inverse, square.shape)
        cross[...] = jnp.broadcast_to(pull, cross.shape)

    lane = lax.broadcasted_iota(jnp.int32, (tokens, per), 1)

    def put(ref, g, hh, value):
        ref[g] = jnp.where(lane == hh, value, ref[g])

    def pulled(g):
        rho_ref[g] = jnp.zeros((tokens, per), F32)

        def pair_at(hh):
            right = []
            for at in range(2):
                head = g * per + hh + at
                row = pl.ds(head, 1)
                place = pl.ds(pl.multiple_of((hh + at) * tokens, tokens), tokens)
                silu = silus[g, place, :]
                mix = mixed[head]
                gated = mix * silu
                natural = pl.ds(hh + at, tokens, stride=per)
                cot = cots[g, natural, :]
                inverse = square[...]
                ggain[row, :] = jnp.sum(cot * gated * inverse, axis=0, keepdims=True)
                grad_gated = inverse * (cot * gains[g, pl.ds(hh + at, 1), :]) - cross[...] * gated
                grad_mix = grad_gated * silu
                cots[g, natural, :] = grad_gated * mix * slopes[g, place, :]
                x_one = xh[head].astype(F32)
                skip = skip_line[row, :]
                gskip[row, :] = jnp.sum(grad_mix * x_one, axis=0, keepdims=True)
                put(
                    rho_ref,
                    g,
                    hh + at,
                    jnp.sum(grad_mix * (mix - x_one * skip), axis=1, keepdims=True),
                )
                mixed[head] = grad_mix * skip
                high, low = split(grad_mix * erb[head])
                y_high[head] = high
                y_low[head] = low
                right.append(tall([high, low]))
            back = dot(ctct[g], wide(right))
            for at in range(2):
                head = g * per + hh + at
                local[head] = back[:, at * dim : (at + 1) * dim] * ec_ref[pl.ds(head, 1), :]

        loop(half // 2, lambda i: pair_at((1 - c) * half + 2 * i))
        first_swap(True, g).start()
        loop(half // 2, lambda i: pair_at(c * half + 2 * i))

    def gate_copy(g):
        place = pl.ds(g * per, per)
        return pltpu.make_async_copy(
            gate_in.at[:, place, :], ggate_hbm.at[:, place, :], out_sem.at[g]
        )

    def x_copy(g):
        place = pl.ds(g * per, per)
        return pltpu.make_async_copy(
            x_in.at[:, place, :], gx_hbm.at[:, place, :], out_sem.at[groups + g]
        )

    def inner_part(g, hh, grad_scaled):
        for at in range(2):
            head = g * per + hh + at
            inner = grad_scaled[:, at * dim : (at + 1) * dim] * esb[head]
            put(
                sigma_ref,
                g,
                hh + at,
                jnp.sum(inner * xh[head].astype(F32), axis=1, keepdims=True),
            )
            yield at, head, inner

    def inside_back(g):
        gate_in[:, g * per : (g + 1) * per, :] = cots[g].reshape(tokens, per, dim).astype(BF16)
        gate_copy(g).start()
        grad_m[...] = jnp.zeros_like(grad_m)
        grad_c[...] = jnp.zeros_like(grad_c)

        def pair_at(i):
            hh = 2 * i
            head = g * per + hh
            yh = wide([y_high[head], y_high[head + 1]])
            yl = wide([y_low[head], y_low[head + 1]])
            x_high = wide([xs_high[head], xs_high[head + 1]])
            x_low = wide([xs_low[head], xs_low[head + 1]])
            left = wide([yh, yh, yl])
            grad_m[...] += dot_nt(left, wide([x_high, x_low, x_high]))
            s_high, s_low = split(
                wide(
                    [carried[head + at] * ec_ref[pl.ds(head + at, 1), :] for at in range(2)]
                )
            )
            grad_c[...] += dot_nt(left, wide([s_high, s_low, s_high]))
            grad_scaled = dot(causal_t[g], tall([yh, yl, yh]))
            for at in range(2):
                one = head + at
                inner = grad_scaled[:, at * dim : (at + 1) * dim] * esb[one]
                put(
                    sigma_ref,
                    g,
                    hh + at,
                    jnp.sum(inner * xh[one].astype(F32), axis=1, keepdims=True),
                )
                mixed[one] += inner
                decay = ec_ref[pl.ds(one, 1), :]
                fresh[one] += (decay * decay) * carried[one]

        sigma_ref[g] = jnp.zeros((tokens, per), F32)
        loop(per // 2, pair_at)
        value = jnp.where(lower(tokens), grad_m[...], 0.0)
        high, low = split(value)
        part = grad_c[...] + dot(wide([high, low]), tall([bb[g, :, :dim], bb[g, :, :dim]]))
        halves[pl.ds(g, tokens, stride=groups), :] = part
        high, low = split(jnp.transpose(value))
        grad_b[g] = dot(wide([high, low]), tall([cc[g, :, :dim], cc[g, :, :dim]]))

    def last(g):
        wide_x = silus.at[g]

        def pair_at(i):
            hh = 2 * i
            head = g * per + hh
            parts = []
            for at in range(2):
                one = head + at
                decay = ec_ref[pl.ds(one, 1), :]
                rows[pl.ds(one, 1), :] = jnp.sum(behind[one] * fresh[one], axis=0, keepdims=True)
                parts.append(behind[one] * decay)
            s_high, s_low = split(wide(parts))
            x_high = wide([xs_high[head], xs_high[head + 1]])
            x_low = wide([xs_low[head], xs_low[head + 1]])
            grad_b[g] += dot_nt(wide([x_high, x_high, x_low]), wide([s_high, s_low, s_high]))
            grad_scaled = dot(bb[g], tall([s_high, s_low]))
            for at in range(2):
                one = head + at
                inner = grad_scaled[:, at * dim : (at + 1) * dim] * esb[one]
                more = jnp.sum(inner * xh[one].astype(F32), axis=1, keepdims=True)
                sigma_ref[g] += jnp.where(lane == hh + at, more, 0.0)
                wide_x[pl.ds(hh + at, tokens, stride=per), :] = mixed[one] + inner

        loop(per // 2, pair_at)
        x_in[:, g * per : (g + 1) * per, :] = wide_x[...].reshape(tokens, per, dim).astype(BF16)
        x_copy(g).start()
        here = slice(g * per, (g + 1) * per)
        sums = lax.dot_general(
            rho_ref[g] - sigma_ref[g],
            jnp.where(lower(tokens), 1.0, 0.0).astype(F32),
            (((0,), (0,)), ((), ())),
            precision=HIGH,
            preferred_element_type=F32,
        )
        grad_log = sums + jnp.sum(rows[here, :], axis=1, keepdims=True)
        bias_here = column(bias_ref)[here]
        rate_here = -jnp.exp(column(a_ref)[here])
        value = dt_ref[here, :].astype(F32) + bias_here
        step_here = softplus(value)
        grad_dt = (jnp.transpose(sigma_ref[g]) / step_here + grad_log * rate_here) * sigmoid(value)
        gdt_ref[here, :] = grad_dt.astype(BF16)
        return (
            jnp.sum(grad_log * step_here, axis=1, keepdims=True) * rate_here,
            jnp.sum(grad_dt, axis=1, keepdims=True),
            jnp.sum(gskip[here, :], axis=1, keepdims=True),
        )

    def swap_copy(source, target, sems):
        return pltpu.make_async_remote_copy(
            src_ref=source,
            dst_ref=target,
            send_sem=sems[0].at[1],
            recv_sem=sems[1].at[1],
            device_id={"fsdp": other},
            device_id_type=MESH,
        )

    def all_copy(ref, sems, hop):
        return pltpu.make_async_remote_copy(
            src_ref=ref.at[0],
            dst_ref=ref.at[hop],
            send_sem=sems[0].at[1 + hop],
            recv_sem=sems[1].at[1 + hop],
            device_id={"ctx": lax.rem(me + hop, count)},
            device_id_type=MESH,
        )

    gain_sems, small_sems = (gain_send, gain_recv), (small_send, small_recv)

    def gain_swap_copy():
        return swap_copy(
            ggain.at[pl.ds(pl.multiple_of(other * per, per), per)], gain_swap, gain_sems
        )

    copy_in(0).wait()
    states(0)
    for hop in range(1, ring_len):
        decay_copy(hop).wait()
    combine(False, 0)
    states(1)
    combine(False, 1)
    scores(0)
    scores(1)
    inside(0)
    copy_in(1).wait()
    copy_in(2).wait()
    prefixes(False, 0)
    widen(0)
    second_chips(False, 0)
    inside(1)
    prefixes(False, 1)
    widen(1)
    second_chips(False, 1)
    gain_copy().wait()
    returned(False, 0)
    second_swap(False, 0).wait()
    gated_norm(0)
    pulled(0)
    returned(False, 1)
    combine(True, 0)
    second_swap(False, 1).wait()
    gated_norm(1)
    prefixes(True, 0)
    pulled(1)
    second_chips(True, 0)
    combine(True, 1)
    gain_swap_copy().start()
    inside_back(0)
    returned(True, 0)
    prefixes(True, 1)
    gain_swap_copy().wait()
    gain_all[0] = gain_swap[...] + ggain[pl.ds(pl.multiple_of(mine * per, per), per), :]
    for hop in range(1, count):
        all_copy(gain_all, gain_sems, hop).start()
    inside_back(1)
    gc_ref[...] = halves[...].astype(BF16)
    second_chips(True, 1)
    second_swap(True, 0).wait()
    sums = [last(0)]
    returned(True, 1)
    second_swap(True, 1).wait()
    sums.append(last(1))
    turn = lax.broadcasted_iota(jnp.int32, (per, dim), 0) == lax.broadcasted_iota(
        jnp.int32, (per, dim), 1
    )
    shifted = lax.broadcasted_iota(jnp.int32, (per, dim), 0) + per == lax.broadcasted_iota(
        jnp.int32, (per, dim), 1
    )
    small_all[0] = jnp.zeros(small_out.shape, F32)
    for at in range(3):
        small_all[0, at : at + 1, :] = jnp.sum(
            jnp.where(turn, sums[0][at], 0.0) + jnp.where(shifted, sums[1][at], 0.0),
            axis=0,
            keepdims=True,
        )
    small_mine = swap_copy(small_all.at[0], small_swap, small_sems)
    small_mine.start()
    for g in range(groups):
        halves[pl.ds(g, tokens, stride=groups), :] = grad_b[g]
    gb_ref[...] = halves[...].astype(BF16)
    for hop in range(1, count):
        all_copy(gain_all, gain_sems, hop).wait()
    gain_total = gain_all[0]
    for hop in range(1, count):
        gain_total = gain_total + gain_all[hop]
    gain_out[...] = gain_total * scale
    small_mine.wait()
    small_all[0] += small_swap[...]
    for hop in range(1, count):
        all_copy(small_all, small_sems, hop).start()
    for hop in range(1, count):
        all_copy(small_all, small_sems, hop).wait()
    small_total = small_all[0]
    for hop in range(1, count):
        small_total = small_total + small_all[hop]
    small_out[...] = small_total * scale
    for g in range(groups):
        gate_copy(g).wait()
        x_copy(g).wait()


def per_device(
    x_input,
    gate_input,
    dt_raw,
    b_input,
    c_input,
    a_log,
    dt_bias,
    skip_weight,
    norm_gain,
    valid_len,
    grad_output,
):
    _, tokens, heads, dim = x_input.shape
    groups, state = b_input.shape[2:]
    per = heads // groups
    half = per // CORES
    own = half // RING
    count = lax.axis_size("ctx")
    ring_len = RING * CORES
    shape = jax.ShapeDtypeStruct
    whole = pl.BlockSpec(memory_space=pltpu.VMEM)
    anywhere = pl.BlockSpec(memory_space=pl.ANY)
    limit = valid_len - lax.axis_index("ctx") * tokens
    scale = 1.0 / math.sqrt(tokens * count * lax.axis_size("fsdp"))
    sems = pltpu.SemaphoreType.DMA

    def vmem(*dims, kind=F32):
        return pltpu.VMEM(dims, kind)

    scratch = [
        vmem(tokens, heads, dim, kind=BF16),
        vmem(tokens, heads, dim, kind=BF16),
        vmem(tokens, heads, dim, kind=BF16),
        vmem(heads, tokens, dim, kind=BF16),
        vmem(heads, tokens, dim, kind=BF16),
        vmem(heads, tokens, dim, kind=BF16),
        vmem(heads, tokens, dim),
        vmem(heads, tokens, dim),
        vmem(groups, tokens * per, dim),
        vmem(groups, tokens * per, dim),
        vmem(groups, tokens * per, dim),
        vmem(heads, tokens, dim),
        vmem(heads, tokens, dim, kind=BF16),
        vmem(heads, tokens, dim, kind=BF16),
        vmem(heads, state, dim),
        vmem(heads, state, dim),
        vmem(heads, state, dim),
        vmem(heads, state, dim),
        vmem(groups * half, state, dim),
        vmem(groups * half, state, dim),
        vmem(groups * half, state, dim),
        vmem(groups * half, state, dim),
        vmem(groups * half, state, dim),
        vmem(groups * own, state, dim),
        vmem(groups * own, state, dim),
        vmem(groups, tokens, 3 * tokens, kind=BF16),
        vmem(groups, tokens, 3 * tokens, kind=BF16),
        vmem(groups, state, 2 * tokens, kind=BF16),
        vmem(groups, tokens, 2 * state, kind=BF16),
        vmem(groups, tokens, 2 * state, kind=BF16),
        vmem(groups, state, 2 * tokens, kind=BF16),
        vmem(heads, dim),
        vmem(ring_len, heads, dim),
        vmem(groups, per, dim),
        vmem(heads, dim),
        vmem(8, dim),
        vmem(groups, tokens, per),
        vmem(groups, tokens, per),
        vmem(tokens, dim),
        vmem(tokens, dim),
        vmem(tokens, tokens),
        vmem(tokens, state),
        vmem(groups, tokens, state),
        vmem(tokens * groups, state),
        vmem(heads, dim),
        vmem(heads, dim),
        vmem(heads, dim),
        vmem(per, dim),
        vmem(count, per, dim),
        vmem(8, dim),
        vmem(count, 8, dim),
        sems((3,)),
        sems((2 * groups,)),
        sems((ring_len,)),
        sems((ring_len,)),
        sems((2 * groups * 9,)),
        sems((2 * groups * 9,)),
        sems((1 + count,)),
        sems((1 + count,)),
        sems((1 + count,)),
        sems((1 + count,)),
    ]
    grad_x, ggate, grad_dt, grad_b, grad_c, small, gain = pl.pallas_call(
        functools.partial(mixer_kernel, scale, groups),
        in_specs=[pl.BlockSpec(memory_space=pltpu.SMEM), anywhere, anywhere, anywhere] + [whole] * 7,
        out_specs=[anywhere, anywhere] + [whole] * 5,
        out_shape=[
            shape((tokens, heads, dim), BF16),
            shape((tokens, heads, dim), BF16),
            shape((heads, tokens), BF16),
            shape((tokens * groups, state), BF16),
            shape((tokens * groups, state), BF16),
            shape((8, dim), F32),
            shape((per, dim), F32),
        ],
        scratch_shapes=scratch,
        compiler_params=pltpu.CompilerParams(
            collective_id=0, has_side_effects=True, vmem_limit_bytes=VMEM_LIMIT
        ),
        name="mixer",
    )(
        limit,
        x_input[0],
        gate_input[0],
        grad_output[0],
        dt_raw[0],
        b_input.reshape(tokens * groups, state),
        c_input.reshape(tokens * groups, state),
        a_log.reshape(1, heads),
        dt_bias.reshape(1, heads),
        skip_weight.reshape(1, heads),
        norm_gain.reshape(per, dim),
    )
    return (
        grad_x[None],
        ggate[None],
        grad_dt[None],
        grad_b.reshape(b_input.shape),
        grad_c.reshape(c_input.shape),
        small[0, :heads],
        small[1, :heads],
        small[2, :heads],
        gain.reshape(norm_gain.shape),
    )


def solution(mesh):
    placed = (
        P("fsdp", "ctx", "tp", None),
        P("fsdp", "ctx", "tp", None),
        P("fsdp", "tp", "ctx"),
        P("fsdp", "ctx", "tp", None),
        P("fsdp", "ctx", "tp", None),
        P("tp"),
        P("tp"),
        P("tp"),
        P(("tp", "fsdp")),
        P("fsdp"),
        P("fsdp", "ctx", "tp", None),
    )
    return jax.shard_map(
        per_device,
        mesh=mesh,
        in_specs=placed,
        out_specs=(
            P("fsdp", "ctx", "tp", None),
            P("fsdp", "ctx", "tp", None),
            P("fsdp", "tp", "ctx"),
            P("fsdp", "ctx", "tp", None),
            P("fsdp", "ctx", "tp", None),
            P("tp"),
            P("tp"),
            P("tp"),
            P(("tp", "fsdp")),
        ),
        check_vma=False,
    )
```

```python
import functools
import math

import jax
import jax.numpy as jnp
from jax import lax
from jax.experimental import pallas as pl
from jax.experimental.pallas import tpu as pltpu
from jax.sharding import PartitionSpec as P

EPS = 1e-05
F32 = jnp.float32
BF16 = jnp.bfloat16
MESH = pl.DeviceIdType.MESH
VMEM_LIMIT = 60 * 1024 * 1024
RING, CORES = 4, 2


def split(value):
    high = value.astype(BF16)
    return high, (value - high.astype(F32)).astype(BF16)


def dot(left, right):
    return jnp.dot(left, right, preferred_element_type=F32)


def dot_ones(value, ones):
    high, low = split(value)
    lowest = (value - high.astype(F32) - low.astype(F32)).astype(BF16)
    return dot(high, ones) + dot(low, ones) + dot(lowest, ones)


def dot_nt(left, right):
    return lax.dot_general(left, right, (((1,), (1,)), ((), ())), preferred_element_type=F32)


def softplus(value):
    return jnp.maximum(value, 0.0) + jnp.log1p(jnp.exp(-jnp.abs(value)))


def sigmoid(value):
    return 1.0 / (1.0 + jnp.exp(-value))


def lower(length):
    row = lax.broadcasted_iota(jnp.int32, (length, length), 0)
    column = lax.broadcasted_iota(jnp.int32, (length, length), 1)
    return row >= column


def loop(count, body):
    def one(at, carry):
        body(at)
        return carry

    lax.fori_loop(0, count, one, 0)


def wide(parts):
    return jnp.concatenate(parts, axis=1)


def tall(parts):
    return jnp.concatenate(parts, axis=0)


def mixer_kernel(
    scale,
    groups,
    limit_ref,
    x_hbm,
    gate_hbm,
    out_hbm,
    dt_ref,
    b_ref,
    c_ref,
    a_ref,
    bias_ref,
    skip_ref,
    gain_ref,
    gx_hbm,
    ggate_hbm,
    gdt_ref,
    gb_ref,
    gc_ref,
    small_out,
    gain_out,
    x_in,
    gate_in,
    out_in,
    xh,
    xs_high,
    xs_low,
    esb,
    erb,
    cots,
    silus,
    slopes,
    mixed,
    y_high,
    y_low,
    fresh,
    carried,
    local,
    behind,
    sib,
    pair,
    scat,
    pref,
    ret,
    total,
    ztotal,
    causal_m,
    causal_t,
    bt,
    bb,
    cc,
    ctct,
    ec_ref,
    decays,
    gains,
    skip_line,
    decay_rows,
    rho_ref,
    sigma_ref,
    square,
    cross,
    grad_m,
    grad_c,
    grad_b,
    halves,
    ggain,
    gskip,
    rows,
    gain_swap,
    gain_all,
    small_swap,
    small_all,
    in_sem,
    out_sem,
    decay_send,
    decay_recv,
    send_sem,
    recv_sem,
    gain_send,
    gain_recv,
    small_send,
    small_recv,
):
    tokens, heads, dim = x_in.shape
    per = heads // groups
    half = per // CORES
    own = half // RING
    count = lax.axis_size("ctx")
    me = lax.axis_index("ctx")
    ring_len = RING * CORES
    z = me // ring_len
    q = lax.rem(me, ring_len)
    y = q // CORES
    c = lax.rem(q, CORES)
    mine = lax.axis_index("fsdp")
    other = 1 - mine

    def copy_in(at, g):
        source, target = ((x_hbm, x_in), (gate_hbm, gate_in), (out_hbm, out_in))[at]
        place = pl.ds(g * per, per)
        return pltpu.make_async_copy(
            source.at[:, place, :], target.at[:, place, :], in_sem.at[at * groups + g]
        )

    for at in range(3):
        for g in range(groups):
            copy_in(at, g).start()
    barrier = pltpu.get_barrier_semaphore()
    far = [
        {"fsdp": other},
        {"ctx": (1 - z) * ring_len + q},
        {"ctx": (1 - z) * ring_len + q, "fsdp": other},
    ]
    for peer in (far[0], far[2]):
        pl.semaphore_signal(barrier, inc=1, device_id=peer, device_id_type=MESH)
    for hop in range(1, count):
        pl.semaphore_signal(
            barrier, inc=1, device_id={"ctx": lax.rem(me + hop, count)}, device_id_type=MESH
        )

    diagonal = lax.broadcasted_iota(jnp.int32, (heads, heads), 0) == lax.broadcasted_iota(
        jnp.int32, (heads, heads), 1
    )

    def column(ref):
        return jnp.sum(jnp.where(diagonal, ref[...], 0.0), axis=1, keepdims=True)

    rate = -jnp.exp(column(a_ref))
    bias = column(bias_ref)
    skip_line[...] = jnp.broadcast_to(column(skip_ref), skip_line.shape)
    step = softplus(dt_ref[...].astype(F32) + bias)
    row = lax.broadcasted_iota(jnp.int32, (tokens, tokens), 0)
    upto = row <= lax.broadcasted_iota(jnp.int32, (tokens, tokens), 1)
    running = dot_ones(step * rate, jnp.where(upto, 1.0, 0.0).astype(BF16))
    middle = 0.5 * running[:, tokens - 1 :]
    er = jnp.transpose(jnp.exp(running - middle))
    es = jnp.transpose(jnp.exp(middle - running) * step)
    ec = jnp.exp(middle)
    ec_ref[...] = jnp.broadcast_to(ec, ec_ref.shape)
    own_lane = lax.broadcasted_iota(jnp.int32, (heads, dim), 0) == lax.broadcasted_iota(
        jnp.int32, (heads, dim), 1
    )
    decay_row = jnp.sum(jnp.where(own_lane, ec * ec, 0.0), axis=0, keepdims=True)
    decay_rows[q] = jnp.broadcast_to(decay_row, decay_rows.shape[1:])

    def decay_copy(hop):
        return pltpu.make_async_remote_copy(
            src_ref=decay_rows.at[q],
            dst_ref=decay_rows.at[q],
            send_sem=decay_send.at[hop],
            recv_sem=decay_recv.at[hop],
            device_id={"ctx": z * ring_len + lax.rem(q + hop, ring_len)},
            device_id_type=MESH,
        )

    def gain_copy():
        return pltpu.make_async_remote_copy(
            src_ref=gain_ref,
            dst_ref=gains.at[mine],
            send_sem=gain_send.at[0],
            recv_sem=gain_recv.at[0],
            device_id={"fsdp": other},
            device_id_type=MESH,
        )

    gains[mine] = gain_ref[...]

    halves[...] = b_ref[...].astype(F32)
    b_groups = [halves[pl.ds(g, tokens, stride=groups), :] for g in range(groups)]
    halves[...] = c_ref[...].astype(F32)
    c_groups = [halves[pl.ds(g, tokens, stride=groups), :] for g in range(groups)]
    for g in range(groups):
        b_one, c_one = b_groups[g].astype(BF16), c_groups[g].astype(BF16)
        b_turn = jnp.transpose(b_groups[g]).astype(BF16)
        c_turn = jnp.transpose(c_groups[g]).astype(BF16)
        bt[g] = wide([b_turn, b_turn])
        bb[g] = wide([b_one, b_one])
        cc[g] = wide([c_one, c_one])
        ctct[g] = wide([c_turn, c_turn])

    def remote(later, g, which, source, target, device):
        at = (int(later) * groups + g) * 9 + which
        return pltpu.make_async_remote_copy(
            src_ref=source,
            dst_ref=target,
            send_sem=send_sem.at[at],
            recv_sem=recv_sem.at[at],
            device_id={"ctx": device},
            device_id_type=MESH,
        )

    sibling = z * ring_len + y * CORES + (1 - c)

    def ring_device(hop):
        return z * ring_len + lax.rem(y + hop, RING) * CORES + c

    def first_swap(later, g):
        source = local if later else fresh
        return remote(
            later,
            g,
            0,
            source.at[pl.ds(g * per + (1 - c) * half, half)],
            sib.at[pl.ds(g * half, half)],
            sibling,
        )

    def scatter(later, g, hop):
        to = lax.rem(y + hop, RING)
        return remote(
            later,
            g,
            hop,
            pair.at[pl.ds(g * half + to * own, own)],
            scat.at[pl.ds(g * half + y * own, own)],
            ring_device(hop),
        )

    def cross_z(later, g):
        return remote(
            later,
            g,
            7,
            total.at[pl.ds(g * own, own)],
            ztotal.at[pl.ds(g * own, own)],
            (1 - z) * ring_len + q,
        )

    def give_back(later, g, hop):
        to = lax.rem(y + hop, RING)
        return remote(
            later,
            g,
            3 + hop,
            pref.at[pl.ds(g * half + to * own, own)],
            ret.at[pl.ds(g * half + y * own, own)],
            ring_device(hop),
        )

    def second_swap(later, g):
        target = behind if later else carried
        return remote(
            later,
            g,
            8,
            ret.at[pl.ds(g * half, half)],
            target.at[pl.ds(g * per + c * half, half)],
            sibling,
        )

    def combine(later, g):
        source = local if later else fresh
        second = 0 if later else 1
        first_swap(later, g).wait()

        def one(k):
            head = g * per + c * half + k
            decay = decays[y * CORES + second, pl.ds(head, 1), :]
            is_second = c == second
            mul_own = jnp.where(is_second, 1.0, decay)
            mul_sib = jnp.where(is_second, decay, 1.0)
            value = source[head] * mul_own + sib[g * half + k] * mul_sib
            pair[g * half + k] = value

        loop(half, one)
        for hop in range(1, RING):
            scatter(later, g, hop).start()
        for j in range(own):
            scat[g * half + y * own + j] = pair[g * half + y * own + j]

    def prefixes(later, g):
        for hop in range(1, RING):
            scatter(later, g, hop).wait()
        order = list(range(RING))[:: -1 if later else 1]
        for j in range(own):
            head = g * per + c * half + y * own + j
            state = jnp.zeros_like(scat[0])
            for chip in order:
                decay = decays[chip * CORES, pl.ds(head, 1), :] * decays[chip * CORES + 1, pl.ds(head, 1), :]
                pref[g * half + chip * own + j] = state
                state = scat[g * half + chip * own + j] + decay * state
            total[g * own + j] = state

        @pl.when(z == (1 if later else 0))
        def _():
            cross_z(later, g).start()
            for hop in range(1, RING):
                give_back(later, g, hop).start()

    def second_chips(later, g):
        @pl.when(z == (0 if later else 1))
        def _():
            cross_z(later, g).wait_recv()
            order = list(range(RING))[:: -1 if later else 1]
            for j in range(own):
                head = g * per + c * half + y * own + j
                state = ztotal[g * own + j]
                for chip in order:
                    decay = decays[chip * CORES, pl.ds(head, 1), :] * decays[chip * CORES + 1, pl.ds(head, 1), :]
                    pref[g * half + chip * own + j] += state
                    state = decay * state
            for hop in range(1, RING):
                give_back(later, g, hop).start()

    def returned(later, g):
        source = local if later else fresh
        target = behind if later else carried
        first = 1 if later else 0
        for j in range(own):
            ret[g * half + y * own + j] = pref[g * half + y * own + j]
        for hop in range(1, RING):
            give_back(later, g, hop).wait()

        @pl.when(z == (1 if later else 0))
        def _():
            cross_z(later, g).wait_send()

        def one(k):
            head = g * per + c * half + k
            decay = decays[y * CORES + first, pl.ds(head, 1), :]
            is_first = c == first
            before = ret[g * half + k]
            base = jnp.where(is_first, source[head], sib[g * half + k])
            after = base + decay * before
            target[head] = jnp.where(is_first, before, after)
            ret[g * half + k] = jnp.where(is_first, after, before)

        loop(half, one)
        second_swap(later, g).start()

    def states(g):
        temp = cots.at[g]
        temp[...] = x_in[:, g * per : (g + 1) * per, :].astype(F32).reshape(tokens * per, dim)
        for one in range(per):
            esb[g * per + one] = jnp.broadcast_to(
                es[:, g * per + one : g * per + one + 1], (tokens, dim)
            )

        def pair_at(hh):
            scaled = []
            for at in range(2):
                head = g * per + hh + at
                x_one = temp[pl.ds(hh + at, tokens, stride=per), :]
                xh[head] = x_one.astype(BF16)
                high, low = split(x_one * esb[head])
                xs_high[head] = high
                xs_low[head] = low
                scaled.append(tall([high, low]))
            state = dot(bt[g], wide(scaled))
            for at in range(2):
                head = g * per + hh + at
                fresh[head] = state[:, at * dim : (at + 1) * dim] * ec_ref[pl.ds(head, 1), :]

        loop(half // 2, lambda i: pair_at((1 - c) * half + 2 * i))
        if g == 0:
            pl.semaphore_wait(barrier, count + 1)
        first_swap(False, g).start()
        if g == 0:
            for hop in range(1, ring_len):
                decay_copy(hop).start()
            gain_copy().start()
        loop(half // 2, lambda i: pair_at(c * half + 2 * i))

    def scores(g):
        value = jnp.where(lower(tokens), dot(cc[g, :, :dim], bt[g, :, :tokens]), 0.0)
        high, low = split(value)
        causal_m[g] = wide([high, high, low])
        high, low = split(jnp.transpose(value))
        causal_t[g] = wide([high, high, low])

    def widen(g):
        temp = cots.at[g]
        temp[...] = gate_in[:, g * per : (g + 1) * per, :].astype(F32).reshape(tokens * per, dim)

        def one(hh):
            gate = temp[pl.ds(hh, tokens, stride=per), :]
            sig = sigmoid(gate)
            silu = gate * sig
            place = pl.ds(pl.multiple_of(hh * tokens, tokens), tokens)
            silus[g, place, :] = silu
            slopes[g, place, :] = sig + silu * (1.0 - sig)

        loop(per, one)
        keep = lax.broadcasted_iota(jnp.int32, (tokens, 1, 1), 0) < limit_ref[0]
        temp[...] = jnp.where(
            keep, out_in[:, g * per : (g + 1) * per, :].astype(F32), 0.0
        ).reshape(tokens * per, dim)

    def inside(g):
        for one in range(per):
            erb[g * per + one] = jnp.broadcast_to(
                er[:, g * per + one : g * per + one + 1], (tokens, dim)
            )

        def pair_at(i):
            hh = g * per + 2 * i
            right = wide(
                [tall([xs_high[hh + at], xs_low[hh + at], xs_high[hh + at]]) for at in range(2)]
            )
            scanned = dot(causal_m[g], right)
            for at in range(2):
                head = hh + at
                mixed[head] = scanned[:, at * dim : (at + 1) * dim] * erb[head] + xh[head].astype(
                    F32
                ) * skip_line[pl.ds(head, 1), :]

        loop(per // 2, pair_at)

    def gated_norm(g):
        square[...] = jnp.zeros_like(square)
        cross[...] = jnp.zeros_like(cross)

        def pair_at(hh):
            right = []
            for at in range(2):
                head = g * per + hh + at
                right.append(tall(split(carried[head] * ec_ref[pl.ds(head, 1), :])))
            scanned = dot(cc[g], wide(right))
            sum_square, sum_cross = square[...], cross[...]
            for at in range(2):
                head = g * per + hh + at
                mix = mixed[head] + scanned[:, at * dim : (at + 1) * dim] * erb[head]
                mixed[head] = mix
                place = pl.ds(pl.multiple_of((hh + at) * tokens, tokens), tokens)
                gated = mix * silus[g, place, :]
                cot = cots[g, pl.ds(hh + at, tokens, stride=per), :]
                upper = cot * gains[g, pl.ds(hh + at, 1), :]
                sum_square = sum_square + gated * gated
                sum_cross = sum_cross + upper * gated
            square[...] = sum_square
            cross[...] = sum_cross

        loop(half // 2, lambda i: pair_at(c * half + 2 * i))
        second_swap(False, g).wait()
        loop(half // 2, lambda i: pair_at((1 - c) * half + 2 * i))
        width = per * dim
        inverse = lax.rsqrt(jnp.sum(square[...], axis=1, keepdims=True) * (1.0 / width) + EPS)
        pull = inverse * inverse * inverse * (jnp.sum(cross[...], axis=1, keepdims=True) * (1.0 / width))
        square[...] = jnp.broadcast_to(inverse, square.shape)
        cross[...] = jnp.broadcast_to(pull, cross.shape)

    lane = lax.broadcasted_iota(jnp.int32, (tokens, per), 1)

    def put(ref, g, hh, value):
        ref[g] = jnp.where(lane == hh, value, ref[g])

    def pulled(g):
        rho_ref[g] = jnp.zeros((tokens, per), F32)

        def pair_at(hh):
            right = []
            for at in range(2):
                head = g * per + hh + at
                row = pl.ds(head, 1)
                place = pl.ds(pl.multiple_of((hh + at) * tokens, tokens), tokens)
                silu = silus[g, place, :]
                mix = mixed[head]
                gated = mix * silu
                natural = pl.ds(hh + at, tokens, stride=per)
                cot = cots[g, natural, :]
                inverse = square[...]
                ggain[row, :] = jnp.sum(cot * gated * inverse, axis=0, keepdims=True)
                grad_gated = inverse * (cot * gains[g, pl.ds(hh + at, 1), :]) - cross[...] * gated
                grad_mix = grad_gated * silu
                cots[g, natural, :] = grad_gated * mix * slopes[g, place, :]
                x_one = xh[head].astype(F32)
                skip = skip_line[row, :]
                gskip[row, :] = jnp.sum(grad_mix * x_one, axis=0, keepdims=True)
                put(
                    rho_ref,
                    g,
                    hh + at,
                    jnp.sum(grad_mix * (mix - x_one * skip), axis=1, keepdims=True),
                )
                mixed[head] = grad_mix * skip
                high, low = split(grad_mix * erb[head])
                y_high[head] = high
                y_low[head] = low
                right.append(tall([high, low]))
            back = dot(ctct[g], wide(right))
            for at in range(2):
                head = g * per + hh + at
                local[head] = back[:, at * dim : (at + 1) * dim] * ec_ref[pl.ds(head, 1), :]

        loop(half // 2, lambda i: pair_at((1 - c) * half + 2 * i))
        first_swap(True, g).start()
        loop(half // 2, lambda i: pair_at(c * half + 2 * i))

    def gate_copy(g):
        place = pl.ds(g * per, per)
        return pltpu.make_async_copy(
            gate_in.at[:, place, :], ggate_hbm.at[:, place, :], out_sem.at[g]
        )

    def x_copy(g):
        place = pl.ds(g * per, per)
        return pltpu.make_async_copy(
            x_in.at[:, place, :], gx_hbm.at[:, place, :], out_sem.at[groups + g]
        )

    def inside_back(g, part):
        if part == 0:
            gate_in[:, g * per : (g + 1) * per, :] = (
                cots[g].reshape(tokens, per, dim).astype(BF16)
            )
            gate_copy(g).start()
            grad_m[...] = jnp.zeros_like(grad_m)
            grad_c[...] = jnp.zeros_like(grad_c)
            sigma_ref[g] = jnp.zeros((tokens, per), F32)

        def pair_at(i):
            hh = part * half + 2 * i
            head = g * per + hh
            yh = wide([y_high[head], y_high[head + 1]])
            yl = wide([y_low[head], y_low[head + 1]])
            x_high = wide([xs_high[head], xs_high[head + 1]])
            x_low = wide([xs_low[head], xs_low[head + 1]])
            left = wide([yh, yh, yl])
            grad_m[...] += dot_nt(left, wide([x_high, x_low, x_high]))
            s_high, s_low = split(
                wide(
                    [carried[head + at] * ec_ref[pl.ds(head + at, 1), :] for at in range(2)]
                )
            )
            grad_c[...] += dot_nt(left, wide([s_high, s_low, s_high]))
            grad_scaled = dot(causal_t[g], tall([yh, yl, yh]))
            for at in range(2):
                one = head + at
                inner = grad_scaled[:, at * dim : (at + 1) * dim] * esb[one]
                put(
                    sigma_ref,
                    g,
                    hh + at,
                    jnp.sum(inner * xh[one].astype(F32), axis=1, keepdims=True),
                )
                mixed[one] += inner
                decay = ec_ref[pl.ds(one, 1), :]
                fresh[one] += (decay * decay) * carried[one]

        loop(half // 2, pair_at)
        if part == 0:
            return
        value = jnp.where(lower(tokens), grad_m[...], 0.0)
        high, low = split(value)
        part = grad_c[...] + dot(wide([high, low]), tall([bb[g, :, :dim], bb[g, :, :dim]]))
        halves[pl.ds(g, tokens, stride=groups), :] = part
        high, low = split(jnp.transpose(value))
        grad_b[g] = dot(wide([high, low]), tall([cc[g, :, :dim], cc[g, :, :dim]]))

    def last_sums(g):
        def pair_at(hh):
            head = g * per + hh
            parts = []
            for at in range(2):
                one = head + at
                decay = ec_ref[pl.ds(one, 1), :]
                rows[pl.ds(one, 1), :] = jnp.sum(behind[one] * fresh[one], axis=0, keepdims=True)
                parts.append(behind[one] * decay)
            grad_scaled = dot(bb[g], tall(split(wide(parts))))
            for at in range(2):
                one = head + at
                inner = grad_scaled[:, at * dim : (at + 1) * dim] * esb[one]
                more = jnp.sum(inner * xh[one].astype(F32), axis=1, keepdims=True)
                sigma_ref[g] += jnp.where(lane == hh + at, more, 0.0)
                silus[g, pl.ds(hh + at, tokens, stride=per), :] = mixed[one] + inner

        loop(half // 2, lambda i: pair_at(c * half + 2 * i))
        second_swap(True, g).wait()
        loop(half // 2, lambda i: pair_at((1 - c) * half + 2 * i))
        here = slice(g * per, (g + 1) * per)
        sigma_t = jnp.transpose(sigma_ref[g])
        sums = dot_ones(
            jnp.transpose(rho_ref[g]) - sigma_t, jnp.where(lower(tokens), 1.0, 0.0).astype(BF16)
        )
        grad_log = sums + jnp.sum(rows[here, :], axis=1, keepdims=True)
        bias_here = column(bias_ref)[here]
        rate_here = -jnp.exp(column(a_ref)[here])
        value = dt_ref[here, :].astype(F32) + bias_here
        step_here = softplus(value)
        grad_dt = (sigma_t / step_here + grad_log * rate_here) * sigmoid(value)
        gdt_ref[here, :] = grad_dt.astype(BF16)
        return (
            jnp.sum(grad_log * step_here, axis=1, keepdims=True) * rate_here,
            jnp.sum(grad_dt, axis=1, keepdims=True),
            jnp.sum(gskip[here, :], axis=1, keepdims=True),
        )

    def last_x(g):
        x_in[:, g * per : (g + 1) * per, :] = silus[g].reshape(tokens, per, dim).astype(BF16)
        x_copy(g).start()

    def last_b(g):
        def pair_at(i):
            head = g * per + 2 * i
            s_high, s_low = split(
                wide([behind[head + at] * ec_ref[pl.ds(head + at, 1), :] for at in range(2)])
            )
            x_high = wide([xs_high[head], xs_high[head + 1]])
            x_low = wide([xs_low[head], xs_low[head + 1]])
            grad_b[g] += dot_nt(wide([x_high, x_high, x_low]), wide([s_high, s_low, s_high]))

        loop(per // 2, pair_at)

    def near_copy(ref, sems, hop):
        return pltpu.make_async_remote_copy(
            src_ref=ref.at[0],
            dst_ref=ref.at[hop],
            send_sem=sems[0].at[3 + hop],
            recv_sem=sems[1].at[3 + hop],
            device_id={"ctx": z * ring_len + lax.rem(q + hop, ring_len)},
            device_id_type=MESH,
        )

    def far_copy(source, target, sems, at):
        return pltpu.make_async_remote_copy(
            src_ref=source,
            dst_ref=target,
            send_sem=sems[0].at[1 + at],
            recv_sem=sems[1].at[1 + at],
            device_id=far[at],
            device_id_type=MESH,
        )

    gain_sems, small_sems = (gain_send, gain_recv), (small_send, small_recv)

    def gain_far(at):
        owner = mine if at == 1 else other
        return far_copy(
            ggain.at[pl.ds(pl.multiple_of(owner * per, per), per)], gain_swap.at[at], gain_sems, at
        )

    def small_far(at):
        return far_copy(small_all.at[0], small_swap.at[at], small_sems, at)

    copy_in(0, 0).wait()
    states(0)
    for hop in range(1, ring_len):
        decay_copy(hop).wait()
    for at in range(ring_len):
        decays[at] = jnp.broadcast_to(
            jnp.sum(jnp.where(own_lane, decay_rows[at, :1, :], 0.0), axis=1, keepdims=True),
            decays.shape[1:],
        )
    combine(False, 0)
    copy_in(0, 1).wait()
    states(1)
    combine(False, 1)
    scores(0)
    inside(0)
    copy_in(1, 0).wait()
    copy_in(2, 0).wait()
    widen(0)
    prefixes(False, 0)
    scores(1)
    inside(1)
    second_chips(False, 0)
    copy_in(1, 1).wait()
    copy_in(2, 1).wait()
    widen(1)
    gain_copy().wait()
    prefixes(False, 1)
    second_chips(False, 1)
    returned(False, 0)
    gated_norm(0)
    pulled(0)
    combine(True, 0)
    returned(False, 1)
    gated_norm(1)
    pulled(1)
    combine(True, 1)
    for at in range(3):
        gain_far(at).start()
    inside_back(0, 0)
    prefixes(True, 0)
    inside_back(0, 1)
    second_chips(True, 0)
    inside_back(1, 0)
    prefixes(True, 1)
    inside_back(1, 1)
    for at in range(3):
        gain_far(at).wait()
    gain_all[0] = (
        gain_swap[0]
        + gain_swap[1]
        + gain_swap[2]
        + ggain[pl.ds(pl.multiple_of(mine * per, per), per), :]
    )
    second_chips(True, 1)
    returned(True, 0)
    for hop in range(1, ring_len):
        near_copy(gain_all, gain_sems, hop).start()
    sums = [last_sums(0)]
    last_x(0)
    returned(True, 1)
    sums.append(last_sums(1))
    shifted = lax.broadcasted_iota(jnp.int32, (per, dim), 0) + per == lax.broadcasted_iota(
        jnp.int32, (per, dim), 1
    )
    small_all[0] = jnp.zeros(small_out.shape, F32)
    for at in range(3):
        small_all[0, at : at + 1, :] = jnp.sum(
            jnp.where(own_lane[:per], sums[0][at], 0.0) + jnp.where(shifted, sums[1][at], 0.0),
            axis=0,
            keepdims=True,
        )
    for at in range(3):
        small_far(at).start()
    last_x(1)
    last_b(0)
    for at in range(3):
        small_far(at).wait()
    small_all[0] += small_swap[0] + small_swap[1] + small_swap[2]
    for hop in range(1, ring_len):
        near_copy(small_all, small_sems, hop).start()
    last_b(1)
    gc_ref[...] = halves[...].astype(BF16)
    for g in range(groups):
        halves[pl.ds(g, tokens, stride=groups), :] = grad_b[g]
    gb_ref[...] = halves[...].astype(BF16)
    for hop in range(1, ring_len):
        near_copy(gain_all, gain_sems, hop).wait()
    gain_total = gain_all[0]
    for hop in range(1, ring_len):
        gain_total = gain_total + gain_all[hop]
    gain_out[...] = gain_total * scale
    for hop in range(1, ring_len):
        near_copy(small_all, small_sems, hop).wait()
    small_total = small_all[0]
    for hop in range(1, ring_len):
        small_total = small_total + small_all[hop]
    small_out[...] = small_total * scale
    for g in range(groups):
        gate_copy(g).wait()
        x_copy(g).wait()


def store_kernel(gx_in, ggate_in, gdt_in, gb_in, gc_in, small, gain, *refs):
    outs, held, in_sems, out_sems = refs[:9], refs[9], refs[10], refs[11]
    cuts = in_sems.shape[0] // 2
    rows = gx_in.shape[0] // cuts
    jobs = []
    for at, (source, target) in enumerate(((gx_in, outs[0]), (ggate_in, outs[1]))):
        for cut in range(cuts):
            place, one = pl.ds(cut * rows, rows), at * cuts + cut
            jobs.append(
                (
                    pltpu.make_async_copy(source.at[place], held.at[one], in_sems.at[one]),
                    pltpu.make_async_copy(held.at[one], target.at[place], out_sems.at[one]),
                )
            )
    for job in jobs:
        job[0].start()
    for a, b in ((gdt_in, outs[2]), (gb_in, outs[3]), (gc_in, outs[4]), (gain, outs[8])):
        b[...] = a[...]
    for at in range(3):
        outs[5 + at][...] = small[at : at + 1, : outs[5].shape[1]]
    for job in jobs:
        job[0].wait()
        job[1].start()
    for job in jobs:
        job[1].wait()


def per_device(
    x_input,
    gate_input,
    dt_raw,
    b_input,
    c_input,
    a_log,
    dt_bias,
    skip_weight,
    norm_gain,
    valid_len,
    grad_output,
):
    _, tokens, heads, dim = x_input.shape
    groups, state = b_input.shape[2:]
    per = heads // groups
    half = per // CORES
    own = half // RING
    count = lax.axis_size("ctx")
    ring_len = RING * CORES
    shape = jax.ShapeDtypeStruct
    whole = pl.BlockSpec(memory_space=pltpu.VMEM)
    anywhere = pl.BlockSpec(memory_space=pl.ANY)
    limit = valid_len - lax.axis_index("ctx") * tokens
    scale = 1.0 / math.sqrt(tokens * count * lax.axis_size("fsdp"))
    sems = pltpu.SemaphoreType.DMA

    def vmem(*dims, kind=F32):
        return pltpu.VMEM(dims, kind)

    scratch = [
        vmem(tokens, heads, dim, kind=BF16),
        vmem(tokens, heads, dim, kind=BF16),
        vmem(tokens, heads, dim, kind=BF16),
        vmem(heads, tokens, dim, kind=BF16),
        vmem(heads, tokens, dim, kind=BF16),
        vmem(heads, tokens, dim, kind=BF16),
        vmem(heads, tokens, dim),
        vmem(heads, tokens, dim),
        vmem(groups, tokens * per, dim),
        vmem(groups, tokens * per, dim),
        vmem(groups, tokens * per, dim),
        vmem(heads, tokens, dim),
        vmem(heads, tokens, dim, kind=BF16),
        vmem(heads, tokens, dim, kind=BF16),
        vmem(heads, state, dim),
        vmem(heads, state, dim),
        vmem(heads, state, dim),
        vmem(heads, state, dim),
        vmem(groups * half, state, dim),
        vmem(groups * half, state, dim),
        vmem(groups * half, state, dim),
        vmem(groups * half, state, dim),
        vmem(groups * half, state, dim),
        vmem(groups * own, state, dim),
        vmem(groups * own, state, dim),
        vmem(groups, tokens, 3 * tokens, kind=BF16),
        vmem(groups, tokens, 3 * tokens, kind=BF16),
        vmem(groups, state, 2 * tokens, kind=BF16),
        vmem(groups, tokens, 2 * state, kind=BF16),
        vmem(groups, tokens, 2 * state, kind=BF16),
        vmem(groups, state, 2 * tokens, kind=BF16),
        vmem(heads, dim),
        vmem(ring_len, heads, dim),
        vmem(groups, per, dim),
        vmem(heads, dim),
        vmem(ring_len, 8, dim),
        vmem(groups, tokens, per),
        vmem(groups, tokens, per),
        vmem(tokens, dim),
        vmem(tokens, dim),
        vmem(tokens, tokens),
        vmem(tokens, state),
        vmem(groups, tokens, state),
        vmem(tokens * groups, state),
        vmem(heads, dim),
        vmem(heads, dim),
        vmem(heads, dim),
        vmem(3, per, dim),
        vmem(ring_len, per, dim),
        vmem(3, 8, dim),
        vmem(ring_len, 8, dim),
        sems((3 * groups,)),
        sems((2 * groups,)),
        sems((ring_len,)),
        sems((ring_len,)),
        sems((2 * groups * 9,)),
        sems((2 * groups * 9,)),
        sems((3 + ring_len,)),
        sems((3 + ring_len,)),
        sems((3 + ring_len,)),
        sems((3 + ring_len,)),
    ]
    grad_x, ggate, grad_dt, grad_b, grad_c, small, gain = pl.pallas_call(
        functools.partial(mixer_kernel, scale, groups),
        in_specs=[pl.BlockSpec(memory_space=pltpu.SMEM), anywhere, anywhere, anywhere] + [whole] * 7,
        out_specs=[anywhere, anywhere] + [whole] * 5,
        out_shape=[
            shape((tokens, heads, dim), BF16),
            shape((tokens, heads, dim), BF16),
            shape((heads, tokens), BF16),
            shape((tokens * groups, state), BF16),
            shape((tokens * groups, state), BF16),
            shape((8, dim), F32),
            shape((per, dim), F32),
        ],
        scratch_shapes=scratch,
        compiler_params=pltpu.CompilerParams(
            collective_id=0, has_side_effects=True, vmem_limit_bytes=VMEM_LIMIT
        ),
        name="mixer",
    )(
        limit,
        x_input[0],
        gate_input[0],
        grad_output[0],
        dt_raw[0],
        b_input.reshape(tokens * groups, state),
        c_input.reshape(tokens * groups, state),
        a_log.reshape(1, heads),
        dt_bias.reshape(1, heads),
        skip_weight.reshape(1, heads),
        norm_gain.reshape(per, dim),
    )
    made = (grad_x, ggate, grad_dt, grad_b, grad_c)
    line = shape((1, heads), F32)
    cuts = 4
    outs = pl.pallas_call(
        store_kernel,
        in_specs=[anywhere, anywhere] + [whole] * 5,
        out_specs=[anywhere, anywhere] + [whole] * 7,
        out_shape=[shape(a.shape, a.dtype) for a in made] + [line] * 3 + [shape((per, dim), F32)],
        scratch_shapes=[
            vmem(2 * cuts, tokens // cuts, heads, dim, kind=BF16),
            sems((2 * cuts,)),
            sems((2 * cuts,)),
        ],
        name="store",
    )(*made, small, gain)
    return (
        outs[0][None],
        outs[1][None],
        outs[2][None],
        outs[3].reshape(b_input.shape),
        outs[4].reshape(c_input.shape),
        outs[5].reshape(heads),
        outs[6].reshape(heads),
        outs[7].reshape(heads),
        outs[8].reshape(norm_gain.shape),
    )


def solution(mesh):
    placed = (
        P("fsdp", "ctx", "tp", None),
        P("fsdp", "ctx", "tp", None),
        P("fsdp", "tp", "ctx"),
        P("fsdp", "ctx", "tp", None),
        P("fsdp", "ctx", "tp", None),
        P("tp"),
        P("tp"),
        P("tp"),
        P(("tp", "fsdp")),
        P("fsdp"),
        P("fsdp", "ctx", "tp", None),
    )
    return jax.shard_map(
        per_device,
        mesh=mesh,
        in_specs=placed,
        out_specs=(
            P("fsdp", "ctx", "tp", None),
            P("fsdp", "ctx", "tp", None),
            P("fsdp", "tp", "ctx"),
            P("fsdp", "ctx", "tp", None),
            P("fsdp", "ctx", "tp", None),
            P("tp"),
            P("tp"),
            P("tp"),
            P(("tp", "fsdp")),
        ),
        check_vma=False,
    )
```

```python
import functools
import math

import jax
import jax.numpy as jnp
from jax import lax
from jax.experimental import pallas as pl
from jax.experimental.pallas import tpu as pltpu
from jax.sharding import PartitionSpec as P

EPS = 1e-05
F32 = jnp.float32
BF16 = jnp.bfloat16
MESH = pl.DeviceIdType.MESH
VMEM_LIMIT = 60 * 1024 * 1024
RING, CORES = 4, 2


def split(value):
    high = value.astype(BF16)
    return high, (value - high.astype(F32)).astype(BF16)


def dot(left, right):
    return jnp.dot(left, right, preferred_element_type=F32)


def dot_ones(value, ones):
    high, low = split(value)
    lowest = (value - high.astype(F32) - low.astype(F32)).astype(BF16)
    return dot(high, ones) + dot(low, ones) + dot(lowest, ones)


def dot_nt(left, right):
    return lax.dot_general(left, right, (((1,), (1,)), ((), ())), preferred_element_type=F32)


def softplus(value):
    return jnp.maximum(value, 0.0) + jnp.log1p(jnp.exp(-jnp.abs(value)))


def sigmoid(value):
    return 1.0 / (1.0 + jnp.exp(-value))


def lower(length):
    row = lax.broadcasted_iota(jnp.int32, (length, length), 0)
    column = lax.broadcasted_iota(jnp.int32, (length, length), 1)
    return row >= column


def loop(count, body):
    def one(at, carry):
        body(at)
        return carry

    lax.fori_loop(0, count, one, 0)


def wide(parts):
    return jnp.concatenate(parts, axis=1)


def tall(parts):
    return jnp.concatenate(parts, axis=0)


def mixer_kernel(
    scale,
    groups,
    limit_ref,
    x_hbm,
    gate_hbm,
    out_hbm,
    dt_hbm,
    b_hbm,
    c_hbm,
    a_hbm,
    bias_hbm,
    skip_hbm,
    gain_hbm,
    gx_hbm,
    ggate_hbm,
    gdt_hbm,
    gb_hbm,
    gc_hbm,
    small_hbm,
    gain_out_hbm,
    dt_ref,
    b_ref,
    c_ref,
    a_ref,
    bias_ref,
    skip_ref,
    gain_ref,
    gdt_ref,
    gb_ref,
    gc_ref,
    small_out,
    gain_out,
    x_in,
    gate_in,
    out_in,
    xh,
    xs_high,
    xs_low,
    esb,
    erb,
    cots,
    silus,
    slopes,
    mixed,
    y_high,
    y_low,
    fresh,
    carried,
    local,
    behind,
    sib,
    pair,
    scat,
    pref,
    ret,
    total,
    ztotal,
    causal_m,
    causal_t,
    bt,
    bb,
    cc,
    ctct,
    ec_ref,
    decays,
    gains,
    skip_line,
    decay_rows,
    chip_rows,
    chains,
    rho_ref,
    sigma_ref,
    square,
    cross,
    grad_m,
    grad_c,
    grad_b,
    halves,
    ggain,
    gskip,
    rows,
    gain_swap,
    gain_all,
    small_swap,
    small_all,
    in_sem,
    out_sem,
    lead_sem,
    tail_sem,
    decay_send,
    decay_recv,
    send_sem,
    recv_sem,
    gain_send,
    gain_recv,
    small_send,
    small_recv,
):
    tokens, heads, dim = x_in.shape
    per = heads // groups
    half = per // CORES
    own = half // RING
    count = lax.axis_size("ctx")
    me = lax.axis_index("ctx")
    ring_len = RING * CORES
    z = me // ring_len
    q = lax.rem(me, ring_len)
    y = q // CORES
    c = lax.rem(q, CORES)
    mine = lax.axis_index("fsdp")
    other = 1 - mine

    def copy_in(at, g):
        source, target = ((x_hbm, x_in), (gate_hbm, gate_in), (out_hbm, out_in))[at]
        place = pl.ds(g * per, per)
        return pltpu.make_async_copy(
            source.at[:, place, :], target.at[:, place, :], in_sem.at[at * groups + g]
        )

    leads = [
        pltpu.make_async_copy(source, target, lead_sem.at[at])
        for at, (source, target) in enumerate(
            (
                (dt_hbm, dt_ref),
                (a_hbm, a_ref),
                (bias_hbm, bias_ref),
                (skip_hbm, skip_ref),
                (b_hbm, b_ref),
                (gain_hbm, gain_ref),
                (c_hbm, c_ref),
            )
        )
    ]
    tails = [
        pltpu.make_async_copy(source, target, tail_sem.at[at])
        for at, (source, target) in enumerate(
            (
                (gdt_ref, gdt_hbm),
                (gb_ref, gb_hbm),
                (gc_ref, gc_hbm),
                (small_out, small_hbm),
                (gain_out, gain_out_hbm),
            )
        )
    ]
    for lead in leads[:4]:
        lead.start()
    copy_in(0, 0).start()
    for lead in leads[4:]:
        lead.start()
    copy_in(0, 1).start()
    for at in range(1, 3):
        for g in range(groups):
            copy_in(at, g).start()
    barrier = pltpu.get_barrier_semaphore()
    far = [
        {"fsdp": other},
        {"ctx": (1 - z) * ring_len + q},
        {"ctx": (1 - z) * ring_len + q, "fsdp": other},
    ]
    for peer in far:
        pl.semaphore_signal(barrier, inc=1, device_id=peer, device_id_type=MESH)
    for hop in range(1, ring_len):
        pl.semaphore_signal(
            barrier,
            inc=1,
            device_id={"ctx": z * ring_len + lax.rem(q + hop, ring_len)},
            device_id_type=MESH,
        )

    for lead in leads:
        lead.wait()
    diagonal = lax.broadcasted_iota(jnp.int32, (heads, heads), 0) == lax.broadcasted_iota(
        jnp.int32, (heads, heads), 1
    )

    def column(ref):
        return jnp.sum(jnp.where(diagonal, ref[...], 0.0), axis=1, keepdims=True)

    rate = -jnp.exp(column(a_ref))
    bias = column(bias_ref)
    skip_line[...] = jnp.broadcast_to(column(skip_ref), skip_line.shape)
    step = softplus(dt_ref[...].astype(F32) + bias)
    row = lax.broadcasted_iota(jnp.int32, (tokens, tokens), 0)
    upto = row <= lax.broadcasted_iota(jnp.int32, (tokens, tokens), 1)
    running = dot_ones(step * rate, jnp.where(upto, 1.0, 0.0).astype(BF16))
    middle = 0.5 * running[:, tokens - 1 :]
    er = jnp.transpose(jnp.exp(running - middle))
    es = jnp.transpose(jnp.exp(middle - running) * step)
    ec = jnp.exp(middle)
    ec_ref[...] = jnp.broadcast_to(ec, ec_ref.shape)
    own_lane = lax.broadcasted_iota(jnp.int32, (heads, dim), 0) == lax.broadcasted_iota(
        jnp.int32, (heads, dim), 1
    )
    decay_row = jnp.sum(jnp.where(own_lane, ec * ec, 0.0), axis=0, keepdims=True)
    decay_rows[c] = jnp.broadcast_to(decay_row, decay_rows.shape[1:])

    def gain_copy():
        return pltpu.make_async_remote_copy(
            src_ref=gain_ref,
            dst_ref=gains.at[mine],
            send_sem=gain_send.at[0],
            recv_sem=gain_recv.at[0],
            device_id={"fsdp": other},
            device_id_type=MESH,
        )

    gains[mine] = gain_ref[...]

    halves[...] = b_ref[...].astype(F32)
    b_groups = [halves[pl.ds(g, tokens, stride=groups), :] for g in range(groups)]
    halves[...] = c_ref[...].astype(F32)
    c_groups = [halves[pl.ds(g, tokens, stride=groups), :] for g in range(groups)]
    for g in range(groups):
        b_one, c_one = b_groups[g].astype(BF16), c_groups[g].astype(BF16)
        b_turn = jnp.transpose(b_groups[g]).astype(BF16)
        c_turn = jnp.transpose(c_groups[g]).astype(BF16)
        bt[g] = wide([b_turn, b_turn])
        bb[g] = wide([b_one, b_one])
        cc[g] = wide([c_one, c_one])
        ctct[g] = wide([c_turn, c_turn])

    def remote(later, g, which, source, target, device):
        at = (int(later) * groups + g) * 9 + which
        return pltpu.make_async_remote_copy(
            src_ref=source,
            dst_ref=target,
            send_sem=send_sem.at[at],
            recv_sem=recv_sem.at[at],
            device_id={"ctx": device},
            device_id_type=MESH,
        )

    sibling = z * ring_len + y * CORES + (1 - c)

    def ring_device(hop):
        return z * ring_len + lax.rem(y + hop, RING) * CORES + c

    def sibling_decay():
        return pltpu.make_async_remote_copy(
            src_ref=decay_rows.at[c],
            dst_ref=decay_rows.at[c],
            send_sem=decay_send.at[0],
            recv_sem=decay_recv.at[0],
            device_id={"ctx": sibling},
            device_id_type=MESH,
        )

    def chip_decay(hop):
        return pltpu.make_async_remote_copy(
            src_ref=chip_rows.at[y],
            dst_ref=chip_rows.at[y],
            send_sem=decay_send.at[hop],
            recv_sem=decay_recv.at[hop],
            device_id={"ctx": ring_device(hop)},
            device_id_type=MESH,
        )

    def spread(row):
        return jnp.broadcast_to(
            jnp.sum(jnp.where(own_lane, row, 0.0), axis=1, keepdims=True), (heads, dim)
        )

    def core_decays():
        sibling_decay().wait()
        chip_rows[y] = decay_rows[0] * decay_rows[1]
        for hop in range(1, RING):
            chip_decay(hop).start()
        for core in range(CORES):
            decays[core] = spread(decay_rows[core, :1, :])

    def chip_decays():
        for hop in range(1, RING):
            chip_decay(hop).wait()
        for chip in range(RING):
            chains[chip] = spread(chip_rows[chip, :1, :])

    def first_swap(later, g):
        source = local if later else fresh
        return remote(
            later,
            g,
            0,
            source.at[pl.ds(g * per + (1 - c) * half, half)],
            sib.at[pl.ds(g * half, half)],
            sibling,
        )

    def scatter(later, g, hop):
        to = lax.rem(y + hop, RING)
        return remote(
            later,
            g,
            hop,
            pair.at[pl.ds(g * half + to * own, own)],
            scat.at[pl.ds(g * half + y * own, own)],
            ring_device(hop),
        )

    def cross_z(later, g):
        return remote(
            later,
            g,
            7,
            total.at[pl.ds(g * own, own)],
            ztotal.at[pl.ds(g * own, own)],
            (1 - z) * ring_len + q,
        )

    def give_back(later, g, hop):
        to = lax.rem(y + hop, RING)
        return remote(
            later,
            g,
            3 + hop,
            pref.at[pl.ds(g * half + to * own, own)],
            ret.at[pl.ds(g * half + y * own, own)],
            ring_device(hop),
        )

    def second_swap(later, g):
        target = behind if later else carried
        return remote(
            later,
            g,
            8,
            ret.at[pl.ds(g * half, half)],
            target.at[pl.ds(g * per + c * half, half)],
            sibling,
        )

    def combine(later, g):
        source = local if later else fresh
        second = 0 if later else 1
        first_swap(later, g).wait()

        def one(k):
            head = g * per + c * half + k
            decay = decays[second, pl.ds(head, 1), :]
            is_second = c == second
            mul_own = jnp.where(is_second, 1.0, decay)
            mul_sib = jnp.where(is_second, decay, 1.0)
            value = source[head] * mul_own + sib[g * half + k] * mul_sib
            pair[g * half + k] = value

        loop(half, one)
        for hop in range(1, RING):
            scatter(later, g, hop).start()
        for j in range(own):
            scat[g * half + y * own + j] = pair[g * half + y * own + j]

    def prefixes(later, g):
        for hop in range(1, RING):
            scatter(later, g, hop).wait()
        order = list(range(RING))[:: -1 if later else 1]
        for j in range(own):
            head = g * per + c * half + y * own + j
            state = jnp.zeros_like(scat[0])
            for chip in order:
                decay = chains[chip, pl.ds(head, 1), :]
                pref[g * half + chip * own + j] = state
                state = scat[g * half + chip * own + j] + decay * state
            total[g * own + j] = state

        @pl.when(z == (1 if later else 0))
        def _():
            cross_z(later, g).start()
            for hop in range(1, RING):
                give_back(later, g, hop).start()

    def second_chips(later, g):
        @pl.when(z == (0 if later else 1))
        def _():
            cross_z(later, g).wait_recv()
            order = list(range(RING))[:: -1 if later else 1]
            for j in range(own):
                head = g * per + c * half + y * own + j
                state = ztotal[g * own + j]
                for chip in order:
                    decay = chains[chip, pl.ds(head, 1), :]
                    pref[g * half + chip * own + j] += state
                    state = decay * state
            for hop in range(1, RING):
                give_back(later, g, hop).start()

    def returned(later, g):
        source = local if later else fresh
        target = behind if later else carried
        first = 1 if later else 0
        for j in range(own):
            ret[g * half + y * own + j] = pref[g * half + y * own + j]
        for hop in range(1, RING):
            give_back(later, g, hop).wait()

        @pl.when(z == (1 if later else 0))
        def _():
            cross_z(later, g).wait_send()

        def one(k):
            head = g * per + c * half + k
            decay = decays[first, pl.ds(head, 1), :]
            is_first = c == first
            before = ret[g * half + k]
            base = jnp.where(is_first, source[head], sib[g * half + k])
            after = base + decay * before
            target[head] = jnp.where(is_first, before, after)
            ret[g * half + k] = jnp.where(is_first, after, before)

        loop(half, one)
        second_swap(later, g).start()

    def states(g):
        temp = cots.at[g]
        temp[...] = x_in[:, g * per : (g + 1) * per, :].astype(F32).reshape(tokens * per, dim)
        for one in range(per):
            esb[g * per + one] = jnp.broadcast_to(
                es[:, g * per + one : g * per + one + 1], (tokens, dim)
            )

        def pair_at(hh):
            scaled = []
            for at in range(2):
                head = g * per + hh + at
                x_one = temp[pl.ds(hh + at, tokens, stride=per), :]
                xh[head] = x_one.astype(BF16)
                high, low = split(x_one * esb[head])
                xs_high[head] = high
                xs_low[head] = low
                scaled.append(tall([high, low]))
            state = dot(bt[g], wide(scaled))
            for at in range(2):
                head = g * per + hh + at
                fresh[head] = state[:, at * dim : (at + 1) * dim] * ec_ref[pl.ds(head, 1), :]

        loop(half // 2, lambda i: pair_at((1 - c) * half + 2 * i))
        if g == 0:
            pl.semaphore_wait(barrier, ring_len + 2)
            sibling_decay().start()
        first_swap(False, g).start()
        if g == 0:
            gain_copy().start()
        loop(half // 2, lambda i: pair_at(c * half + 2 * i))

    def scores(g):
        value = jnp.where(lower(tokens), dot(cc[g, :, :dim], bt[g, :, :tokens]), 0.0)
        high, low = split(value)
        causal_m[g] = wide([high, high, low])
        high, low = split(jnp.transpose(value))
        causal_t[g] = wide([high, high, low])

    def widen(g):
        temp = cots.at[g]
        temp[...] = gate_in[:, g * per : (g + 1) * per, :].astype(F32).reshape(tokens * per, dim)

        def one(hh):
            gate = temp[pl.ds(hh, tokens, stride=per), :]
            sig = sigmoid(gate)
            silu = gate * sig
            place = pl.ds(pl.multiple_of(hh * tokens, tokens), tokens)
            silus[g, place, :] = silu
            slopes[g, place, :] = sig + silu * (1.0 - sig)

        loop(per, one)
        keep = lax.broadcasted_iota(jnp.int32, (tokens, 1, 1), 0) < limit_ref[0]
        temp[...] = jnp.where(
            keep, out_in[:, g * per : (g + 1) * per, :].astype(F32), 0.0
        ).reshape(tokens * per, dim)

    def inside(g):
        for one in range(per):
            erb[g * per + one] = jnp.broadcast_to(
                er[:, g * per + one : g * per + one + 1], (tokens, dim)
            )

        def pair_at(i):
            hh = g * per + 2 * i
            right = wide(
                [tall([xs_high[hh + at], xs_low[hh + at], xs_high[hh + at]]) for at in range(2)]
            )
            scanned = dot(causal_m[g], right)
            for at in range(2):
                head = hh + at
                mixed[head] = scanned[:, at * dim : (at + 1) * dim] * erb[head] + xh[head].astype(
                    F32
                ) * skip_line[pl.ds(head, 1), :]

        loop(per // 2, pair_at)

    def gated_norm(g):
        square[...] = jnp.zeros_like(square)
        cross[...] = jnp.zeros_like(cross)

        def pair_at(hh):
            right = []
            for at in range(2):
                head = g * per + hh + at
                right.append(tall(split(carried[head] * ec_ref[pl.ds(head, 1), :])))
            scanned = dot(cc[g], wide(right))
            sum_square, sum_cross = square[...], cross[...]
            for at in range(2):
                head = g * per + hh + at
                mix = mixed[head] + scanned[:, at * dim : (at + 1) * dim] * erb[head]
                mixed[head] = mix
                place = pl.ds(pl.multiple_of((hh + at) * tokens, tokens), tokens)
                gated = mix * silus[g, place, :]
                cot = cots[g, pl.ds(hh + at, tokens, stride=per), :]
                upper = cot * gains[g, pl.ds(hh + at, 1), :]
                sum_square = sum_square + gated * gated
                sum_cross = sum_cross + upper * gated
            square[...] = sum_square
            cross[...] = sum_cross

        loop(half // 2, lambda i: pair_at(c * half + 2 * i))
        second_swap(False, g).wait()
        loop(half // 2, lambda i: pair_at((1 - c) * half + 2 * i))
        width = per * dim
        inverse = lax.rsqrt(jnp.sum(square[...], axis=1, keepdims=True) * (1.0 / width) + EPS)
        pull = inverse * inverse * inverse * (jnp.sum(cross[...], axis=1, keepdims=True) * (1.0 / width))
        square[...] = jnp.broadcast_to(inverse, square.shape)
        cross[...] = jnp.broadcast_to(pull, cross.shape)

    lane = lax.broadcasted_iota(jnp.int32, (tokens, per), 1)

    def put(ref, g, hh, values):
        ref[g] = jnp.where(lane == hh, values[0], jnp.where(lane == hh + 1, values[1], ref[g]))

    def pulled(g):
        rho_ref[g] = jnp.zeros((tokens, per), F32)

        def pair_at(hh):
            right, rhos = [], []
            for at in range(2):
                head = g * per + hh + at
                row = pl.ds(head, 1)
                place = pl.ds(pl.multiple_of((hh + at) * tokens, tokens), tokens)
                silu = silus[g, place, :]
                mix = mixed[head]
                gated = mix * silu
                natural = pl.ds(hh + at, tokens, stride=per)
                cot = cots[g, natural, :]
                inverse = square[...]
                ggain[row, :] = jnp.sum(cot * gated * inverse, axis=0, keepdims=True)
                grad_gated = inverse * (cot * gains[g, pl.ds(hh + at, 1), :]) - cross[...] * gated
                grad_mix = grad_gated * silu
                cots[g, natural, :] = grad_gated * mix * slopes[g, place, :]
                x_one = xh[head].astype(F32)
                skip = skip_line[row, :]
                gskip[row, :] = jnp.sum(grad_mix * x_one, axis=0, keepdims=True)
                rhos.append(jnp.sum(grad_mix * (mix - x_one * skip), axis=1, keepdims=True))
                mixed[head] = grad_mix * skip
                high, low = split(grad_mix * erb[head])
                y_high[head] = high
                y_low[head] = low
                right.append(tall([high, low]))
            put(rho_ref, g, hh, rhos)
            back = dot(ctct[g], wide(right))
            for at in range(2):
                head = g * per + hh + at
                local[head] = back[:, at * dim : (at + 1) * dim] * ec_ref[pl.ds(head, 1), :]

        loop(half // 2, lambda i: pair_at((1 - c) * half + 2 * i))
        first_swap(True, g).start()
        loop(half // 2, lambda i: pair_at(c * half + 2 * i))

    def gate_copy(g):
        place = pl.ds(g * per, per)
        return pltpu.make_async_copy(
            gate_in.at[:, place, :], ggate_hbm.at[:, place, :], out_sem.at[g]
        )

    def x_copy(g):
        place = pl.ds(g * per, per)
        return pltpu.make_async_copy(
            x_in.at[:, place, :], gx_hbm.at[:, place, :], out_sem.at[groups + g]
        )

    def inside_back(g, part):
        if part == 0:
            gate_in[:, g * per : (g + 1) * per, :] = (
                cots[g].reshape(tokens, per, dim).astype(BF16)
            )
            gate_copy(g).start()
            grad_m[...] = jnp.zeros_like(grad_m)
            grad_c[...] = jnp.zeros_like(grad_c)
            sigma_ref[g] = jnp.zeros((tokens, per), F32)

        def pair_at(i):
            hh = part * half + 2 * i
            sigmas = []
            head = g * per + hh
            yh = wide([y_high[head], y_high[head + 1]])
            yl = wide([y_low[head], y_low[head + 1]])
            x_high = wide([xs_high[head], xs_high[head + 1]])
            x_low = wide([xs_low[head], xs_low[head + 1]])
            left = wide([yh, yh, yl])
            grad_m[...] += dot_nt(left, wide([x_high, x_low, x_high]))
            s_high, s_low = split(
                wide(
                    [carried[head + at] * ec_ref[pl.ds(head + at, 1), :] for at in range(2)]
                )
            )
            grad_c[...] += dot_nt(left, wide([s_high, s_low, s_high]))
            grad_scaled = dot(causal_t[g], tall([yh, yl, yh]))
            for at in range(2):
                one = head + at
                inner = grad_scaled[:, at * dim : (at + 1) * dim] * esb[one]
                sigmas.append(jnp.sum(inner * xh[one].astype(F32), axis=1, keepdims=True))
                mixed[one] += inner
                decay = ec_ref[pl.ds(one, 1), :]
                fresh[one] += (decay * decay) * carried[one]
            put(sigma_ref, g, hh, sigmas)

        loop(half // 2, pair_at)
        if part == 0:
            return
        value = jnp.where(lower(tokens), grad_m[...], 0.0)
        high, low = split(value)
        part = grad_c[...] + dot(wide([high, low]), tall([bb[g, :, :dim], bb[g, :, :dim]]))
        halves[pl.ds(g, tokens, stride=groups), :] = part
        high, low = split(jnp.transpose(value))
        grad_b[g] = dot(wide([high, low]), tall([cc[g, :, :dim], cc[g, :, :dim]]))

    def last_sums(g):
        def pair_at(hh):
            head = g * per + hh
            parts, more = [], []
            for at in range(2):
                one = head + at
                decay = ec_ref[pl.ds(one, 1), :]
                rows[pl.ds(one, 1), :] = jnp.sum(behind[one] * fresh[one], axis=0, keepdims=True)
                parts.append(behind[one] * decay)
            grad_scaled = dot(bb[g], tall(split(wide(parts))))
            for at in range(2):
                one = head + at
                inner = grad_scaled[:, at * dim : (at + 1) * dim] * esb[one]
                more.append(jnp.sum(inner * xh[one].astype(F32), axis=1, keepdims=True))
                silus[g, pl.ds(hh + at, tokens, stride=per), :] = mixed[one] + inner
            sigma_ref[g] += jnp.where(lane == hh, more[0], jnp.where(lane == hh + 1, more[1], 0.0))

        loop(half // 2, lambda i: pair_at(c * half + 2 * i))
        second_swap(True, g).wait()
        loop(half // 2, lambda i: pair_at((1 - c) * half + 2 * i))
        here = slice(g * per, (g + 1) * per)
        sigma_t = jnp.transpose(sigma_ref[g])
        sums = dot_ones(
            jnp.transpose(rho_ref[g]) - sigma_t, jnp.where(lower(tokens), 1.0, 0.0).astype(BF16)
        )
        grad_log = sums + jnp.sum(rows[here, :], axis=1, keepdims=True)
        bias_here = column(bias_ref)[here]
        rate_here = -jnp.exp(column(a_ref)[here])
        value = dt_ref[here, :].astype(F32) + bias_here
        step_here = softplus(value)
        grad_dt = (sigma_t / step_here + grad_log * rate_here) * sigmoid(value)
        gdt_ref[here, :] = grad_dt.astype(BF16)
        return (
            jnp.sum(grad_log * step_here, axis=1, keepdims=True) * rate_here,
            jnp.sum(grad_dt, axis=1, keepdims=True),
            jnp.sum(gskip[here, :], axis=1, keepdims=True),
        )

    def last_x(g):
        x_in[:, g * per : (g + 1) * per, :] = silus[g].reshape(tokens, per, dim).astype(BF16)
        x_copy(g).start()

    def last_b(g):
        def pair_at(i):
            head = g * per + 2 * i
            s_high, s_low = split(
                wide([behind[head + at] * ec_ref[pl.ds(head + at, 1), :] for at in range(2)])
            )
            x_high = wide([xs_high[head], xs_high[head + 1]])
            x_low = wide([xs_low[head], xs_low[head + 1]])
            grad_b[g] += dot_nt(wide([x_high, x_high, x_low]), wide([s_high, s_low, s_high]))

        loop(per // 2, pair_at)

    def near_copy(ref, sems, hop):
        return pltpu.make_async_remote_copy(
            src_ref=ref.at[0],
            dst_ref=ref.at[hop],
            send_sem=sems[0].at[3 + hop],
            recv_sem=sems[1].at[3 + hop],
            device_id={"ctx": z * ring_len + lax.rem(q + hop, ring_len)},
            device_id_type=MESH,
        )

    def far_copy(source, target, sems, at):
        return pltpu.make_async_remote_copy(
            src_ref=source,
            dst_ref=target,
            send_sem=sems[0].at[1 + at],
            recv_sem=sems[1].at[1 + at],
            device_id=far[at],
            device_id_type=MESH,
        )

    gain_sems, small_sems = (gain_send, gain_recv), (small_send, small_recv)

    def gain_far(at):
        owner = mine if at == 1 else other
        return far_copy(
            ggain.at[pl.ds(pl.multiple_of(owner * per, per), per)], gain_swap.at[at], gain_sems, at
        )

    def small_far(at):
        return far_copy(small_all.at[0], small_swap.at[at], small_sems, at)

    copy_in(0, 0).wait()
    states(0)
    core_decays()
    combine(False, 0)
    copy_in(0, 1).wait()
    states(1)
    combine(False, 1)
    scores(0)
    inside(0)
    copy_in(1, 0).wait()
    copy_in(2, 0).wait()
    widen(0)
    chip_decays()
    prefixes(False, 0)
    scores(1)
    inside(1)
    second_chips(False, 0)
    copy_in(1, 1).wait()
    copy_in(2, 1).wait()
    widen(1)
    gain_copy().wait()
    prefixes(False, 1)
    second_chips(False, 1)
    returned(False, 0)
    gated_norm(0)
    pulled(0)
    combine(True, 0)
    returned(False, 1)
    gated_norm(1)
    pulled(1)
    combine(True, 1)
    prefixes(True, 0)
    for at in range(3):
        gain_far(at).start()
    inside_back(0, 0)
    second_chips(True, 0)
    inside_back(0, 1)
    prefixes(True, 1)
    inside_back(1, 0)
    second_chips(True, 1)
    for at in range(3):
        gain_far(at).wait()
    gain_all[0] = (
        gain_swap[0]
        + gain_swap[1]
        + gain_swap[2]
        + ggain[pl.ds(pl.multiple_of(mine * per, per), per), :]
    )
    for hop in range(1, ring_len):
        near_copy(gain_all, gain_sems, hop).start()
    returned(True, 0)
    inside_back(1, 1)
    sums = [last_sums(0)]
    last_x(0)
    returned(True, 1)
    sums.append(last_sums(1))
    tails[0].start()
    shifted = lax.broadcasted_iota(jnp.int32, (per, dim), 0) + per == lax.broadcasted_iota(
        jnp.int32, (per, dim), 1
    )
    small_all[0] = jnp.zeros(small_out.shape, F32)
    for at in range(3):
        small_all[0, at : at + 1, :] = jnp.sum(
            jnp.where(own_lane[:per], sums[0][at], 0.0) + jnp.where(shifted, sums[1][at], 0.0),
            axis=0,
            keepdims=True,
        )
    for at in range(3):
        small_far(at).start()
    last_x(1)
    last_b(0)
    for at in range(3):
        small_far(at).wait()
    small_all[0] += small_swap[0] + small_swap[1] + small_swap[2]
    for hop in range(1, ring_len):
        near_copy(small_all, small_sems, hop).start()
    last_b(1)
    gc_ref[...] = halves[...].astype(BF16)
    tails[2].start()
    for g in range(groups):
        halves[pl.ds(g, tokens, stride=groups), :] = grad_b[g]
    gb_ref[...] = halves[...].astype(BF16)
    tails[1].start()
    for hop in range(1, ring_len):
        near_copy(gain_all, gain_sems, hop).wait()
    gain_total = gain_all[0]
    for hop in range(1, ring_len):
        gain_total = gain_total + gain_all[hop]
    gain_out[...] = gain_total * scale
    tails[4].start()
    for hop in range(1, ring_len):
        near_copy(small_all, small_sems, hop).wait()
    small_total = small_all[0]
    for hop in range(1, ring_len):
        small_total = small_total + small_all[hop]
    small_out[...] = small_total * scale
    tails[3].start()
    for g in range(groups):
        gate_copy(g).wait()
        x_copy(g).wait()
    for tail in tails:
        tail.wait()


def store_kernel(gx_in, ggate_in, gdt_in, gb_in, gc_in, small_in, gain_in, *refs):
    outs = refs[:9]
    held, gdt, gb, gc, small, gain, lines, in_sems, out_sems = refs[9:]
    cuts = held.shape[0] // 2
    rows = gx_in.shape[0] // cuts
    jobs = []
    for at, (source, target) in enumerate(((gx_in, outs[0]), (ggate_in, outs[1]))):
        for cut in range(cuts):
            place = pl.ds(cut * rows, rows)
            jobs.append((source.at[place], held.at[at * cuts + cut], target.at[place]))
    jobs += [(gdt_in, gdt, outs[2]), (gb_in, gb, outs[3]), (gc_in, gc, outs[4])]
    jobs.append((gain_in, gain, outs[8]))
    count = len(jobs)
    into = [pltpu.make_async_copy(job[0], job[1], in_sems.at[at]) for at, job in enumerate(jobs)]
    away = [pltpu.make_async_copy(job[1], job[2], out_sems.at[at]) for at, job in enumerate(jobs)]
    lead = pltpu.make_async_copy(small_in, small, in_sems.at[count])
    lead.start()
    for copy in into:
        copy.start()
    lead.wait()
    for at in range(3):
        lines[at] = small[at : at + 1, : lines.shape[2]]
        away.append(
            pltpu.make_async_copy(lines.at[at], outs[5 + at], out_sems.at[count + at])
        )
        away[-1].start()
    for at in range(count):
        into[at].wait()
        away[at].start()
    for copy in away:
        copy.wait()


def per_device(
    x_input,
    gate_input,
    dt_raw,
    b_input,
    c_input,
    a_log,
    dt_bias,
    skip_weight,
    norm_gain,
    valid_len,
    grad_output,
):
    _, tokens, heads, dim = x_input.shape
    groups, state = b_input.shape[2:]
    per = heads // groups
    half = per // CORES
    own = half // RING
    count = lax.axis_size("ctx")
    ring_len = RING * CORES
    shape = jax.ShapeDtypeStruct
    anywhere = pl.BlockSpec(memory_space=pl.ANY)
    limit = valid_len - lax.axis_index("ctx") * tokens
    scale = 1.0 / math.sqrt(tokens * count * lax.axis_size("fsdp"))
    sems = pltpu.SemaphoreType.DMA

    def vmem(*dims, kind=F32):
        return pltpu.VMEM(dims, kind)

    scratch = [
        vmem(heads, tokens, kind=BF16),
        vmem(tokens * groups, state, kind=BF16),
        vmem(tokens * groups, state, kind=BF16),
        vmem(1, heads),
        vmem(1, heads),
        vmem(1, heads),
        vmem(per, dim),
        vmem(heads, tokens, kind=BF16),
        vmem(tokens * groups, state, kind=BF16),
        vmem(tokens * groups, state, kind=BF16),
        vmem(8, dim),
        vmem(per, dim),
        vmem(tokens, heads, dim, kind=BF16),
        vmem(tokens, heads, dim, kind=BF16),
        vmem(tokens, heads, dim, kind=BF16),
        vmem(heads, tokens, dim, kind=BF16),
        vmem(heads, tokens, dim, kind=BF16),
        vmem(heads, tokens, dim, kind=BF16),
        vmem(heads, tokens, dim),
        vmem(heads, tokens, dim),
        vmem(groups, tokens * per, dim),
        vmem(groups, tokens * per, dim),
        vmem(groups, tokens * per, dim),
        vmem(heads, tokens, dim),
        vmem(heads, tokens, dim, kind=BF16),
        vmem(heads, tokens, dim, kind=BF16),
        vmem(heads, state, dim),
        vmem(heads, state, dim),
        vmem(heads, state, dim),
        vmem(heads, state, dim),
        vmem(groups * half, state, dim),
        vmem(groups * half, state, dim),
        vmem(groups * half, state, dim),
        vmem(groups * half, state, dim),
        vmem(groups * half, state, dim),
        vmem(groups * own, state, dim),
        vmem(groups * own, state, dim),
        vmem(groups, tokens, 3 * tokens, kind=BF16),
        vmem(groups, tokens, 3 * tokens, kind=BF16),
        vmem(groups, state, 2 * tokens, kind=BF16),
        vmem(groups, tokens, 2 * state, kind=BF16),
        vmem(groups, tokens, 2 * state, kind=BF16),
        vmem(groups, state, 2 * tokens, kind=BF16),
        vmem(heads, dim),
        vmem(CORES, heads, dim),
        vmem(groups, per, dim),
        vmem(heads, dim),
        vmem(CORES, 8, dim),
        vmem(RING, 8, dim),
        vmem(RING, heads, dim),
        vmem(groups, tokens, per),
        vmem(groups, tokens, per),
        vmem(tokens, dim),
        vmem(tokens, dim),
        vmem(tokens, tokens),
        vmem(tokens, state),
        vmem(groups, tokens, state),
        vmem(tokens * groups, state),
        vmem(heads, dim),
        vmem(heads, dim),
        vmem(heads, dim),
        vmem(3, per, dim),
        vmem(ring_len, per, dim),
        vmem(3, 8, dim),
        vmem(ring_len, 8, dim),
        sems((3 * groups,)),
        sems((2 * groups,)),
        sems((7,)),
        sems((5,)),
        sems((ring_len,)),
        sems((ring_len,)),
        sems((2 * groups * 9,)),
        sems((2 * groups * 9,)),
        sems((3 + ring_len,)),
        sems((3 + ring_len,)),
        sems((3 + ring_len,)),
        sems((3 + ring_len,)),
    ]
    grad_x, ggate, grad_dt, grad_b, grad_c, small, gain = pl.pallas_call(
        functools.partial(mixer_kernel, scale, groups),
        in_specs=[pl.BlockSpec(memory_space=pltpu.SMEM), ] + [anywhere] * 10,
        out_specs=[anywhere] * 7,
        out_shape=[
            shape((tokens, heads, dim), BF16),
            shape((tokens, heads, dim), BF16),
            shape((heads, tokens), BF16),
            shape((tokens * groups, state), BF16),
            shape((tokens * groups, state), BF16),
            shape((8, dim), F32),
            shape((per, dim), F32),
        ],
        scratch_shapes=scratch,
        compiler_params=pltpu.CompilerParams(
            collective_id=0, has_side_effects=True, vmem_limit_bytes=VMEM_LIMIT
        ),
        name="mixer",
    )(
        limit,
        x_input[0],
        gate_input[0],
        grad_output[0],
        dt_raw[0],
        b_input.reshape(tokens * groups, state),
        c_input.reshape(tokens * groups, state),
        a_log.reshape(1, heads),
        dt_bias.reshape(1, heads),
        skip_weight.reshape(1, heads),
        norm_gain.reshape(per, dim),
    )
    made = (grad_x, ggate, grad_dt, grad_b, grad_c)
    line = shape((1, heads), F32)
    cuts = 4
    outs = pl.pallas_call(
        store_kernel,
        in_specs=[anywhere] * 7,
        out_specs=[anywhere] * 9,
        out_shape=[shape(a.shape, a.dtype) for a in made] + [line] * 3 + [shape((per, dim), F32)],
        scratch_shapes=[
            vmem(2 * cuts, tokens // cuts, heads, dim, kind=BF16),
            vmem(heads, tokens, kind=BF16),
            vmem(tokens * groups, state, kind=BF16),
            vmem(tokens * groups, state, kind=BF16),
            vmem(8, dim),
            vmem(per, dim),
            vmem(3, 1, heads),
            sems((2 * cuts + 5,)),
            sems((2 * cuts + 7,)),
        ],
        name="store",
    )(*made, small, gain)
    return (
        outs[0][None],
        outs[1][None],
        outs[2][None],
        outs[3].reshape(b_input.shape),
        outs[4].reshape(c_input.shape),
        outs[5].reshape(heads),
        outs[6].reshape(heads),
        outs[7].reshape(heads),
        outs[8].reshape(norm_gain.shape),
    )


def solution(mesh):
    placed = (
        P("fsdp", "ctx", "tp", None),
        P("fsdp", "ctx", "tp", None),
        P("fsdp", "tp", "ctx"),
        P("fsdp", "ctx", "tp", None),
        P("fsdp", "ctx", "tp", None),
        P("tp"),
        P("tp"),
        P("tp"),
        P(("tp", "fsdp")),
        P("fsdp"),
        P("fsdp", "ctx", "tp", None),
    )
    return jax.shard_map(
        per_device,
        mesh=mesh,
        in_specs=placed,
        out_specs=(
            P("fsdp", "ctx", "tp", None),
            P("fsdp", "ctx", "tp", None),
            P("fsdp", "tp", "ctx"),
            P("fsdp", "ctx", "tp", None),
            P("fsdp", "ctx", "tp", None),
            P("tp"),
            P("tp"),
            P("tp"),
            P(("tp", "fsdp")),
        ),
        check_vma=False,
    )
```

```python
import functools
import math

import jax
import jax.numpy as jnp
from jax import lax
from jax.experimental import pallas as pl
from jax.experimental.pallas import tpu as pltpu
from jax.sharding import PartitionSpec as P

EPS = 1e-05
F32 = jnp.float32
BF16 = jnp.bfloat16
MESH = pl.DeviceIdType.MESH
VMEM_LIMIT = 60 * 1024 * 1024
RING, CORES = 4, 2


def split(value):
    high = value.astype(BF16)
    return high, (value - high.astype(F32)).astype(BF16)


def dot(left, right):
    return jnp.dot(left, right, preferred_element_type=F32)


def dot_ones(value, ones):
    high, low = split(value)
    lowest = (value - high.astype(F32) - low.astype(F32)).astype(BF16)
    return dot(high, ones) + dot(low, ones) + dot(lowest, ones)


def dot_nt(left, right):
    return lax.dot_general(left, right, (((1,), (1,)), ((), ())), preferred_element_type=F32)


def softplus(value):
    return jnp.maximum(value, 0.0) + jnp.log1p(jnp.exp(-jnp.abs(value)))


def sigmoid(value):
    return 1.0 / (1.0 + jnp.exp(-value))


def lower(length):
    row = lax.broadcasted_iota(jnp.int32, (length, length), 0)
    column = lax.broadcasted_iota(jnp.int32, (length, length), 1)
    return row >= column


def loop(count, body):
    def one(at, carry):
        body(at)
        return carry

    lax.fori_loop(0, count, one, 0)


def wide(parts):
    return jnp.concatenate(parts, axis=1)


def tall(parts):
    return jnp.concatenate(parts, axis=0)


def mixer_kernel(
    scale,
    groups,
    limit_ref,
    x_hbm,
    gate_hbm,
    out_hbm,
    dt_hbm,
    b_hbm,
    c_hbm,
    a_hbm,
    bias_hbm,
    skip_hbm,
    gain_hbm,
    gx_hbm,
    ggate_hbm,
    gdt_hbm,
    gb_hbm,
    gc_hbm,
    small_hbm,
    gain_out_hbm,
    dt_ref,
    b_ref,
    c_ref,
    a_ref,
    bias_ref,
    skip_ref,
    gain_ref,
    gdt_ref,
    gb_ref,
    gc_ref,
    small_out,
    gain_out,
    x_in,
    gate_in,
    out_in,
    xh,
    xs_high,
    xs_low,
    esb,
    erb,
    cots,
    silus,
    slopes,
    mixed,
    y_high,
    y_low,
    fresh,
    carried,
    local,
    behind,
    sib,
    pair,
    scat,
    pref,
    ret,
    total,
    ztotal,
    causal_m,
    causal_t,
    bt,
    bb,
    cc,
    ctct,
    ec_ref,
    decays,
    gains,
    skip_line,
    decay_rows,
    chip_rows,
    chains,
    rho_ref,
    sigma_ref,
    square,
    cross,
    grad_m,
    grad_c,
    grad_b,
    halves,
    ggain,
    gskip,
    rows,
    gain_swap,
    gain_all,
    small_swap,
    small_all,
    in_sem,
    out_sem,
    lead_sem,
    tail_sem,
    decay_send,
    decay_recv,
    send_sem,
    recv_sem,
    gain_send,
    gain_recv,
    small_send,
    small_recv,
):
    tokens, heads, dim = x_in.shape
    per = heads // groups
    half = per // CORES
    own = half // RING
    count = lax.axis_size("ctx")
    me = lax.axis_index("ctx")
    ring_len = RING * CORES
    z = me // ring_len
    q = lax.rem(me, ring_len)
    y = q // CORES
    c = lax.rem(q, CORES)
    mine = lax.axis_index("fsdp")
    other = 1 - mine

    def copy_in(at, g):
        source, target = ((x_hbm, x_in), (gate_hbm, gate_in), (out_hbm, out_in))[at]
        place = pl.ds(g * per, per)
        return pltpu.make_async_copy(
            source.at[:, place, :], target.at[:, place, :], in_sem.at[at * groups + g]
        )

    leads = [
        pltpu.make_async_copy(source, target, lead_sem.at[at])
        for at, (source, target) in enumerate(
            (
                (dt_hbm, dt_ref),
                (a_hbm, a_ref),
                (bias_hbm, bias_ref),
                (skip_hbm, skip_ref),
                (b_hbm, b_ref),
                (gain_hbm, gain_ref),
                (c_hbm, c_ref),
            )
        )
    ]
    tails = [
        pltpu.make_async_copy(source, target, tail_sem.at[at])
        for at, (source, target) in enumerate(
            (
                (gdt_ref, gdt_hbm),
                (gb_ref, gb_hbm),
                (gc_ref, gc_hbm),
                (small_out, small_hbm),
                (gain_out, gain_out_hbm),
            )
        )
    ]
    for lead in leads[:4]:
        lead.start()
    copy_in(0, 0).start()
    for lead in leads[4:]:
        lead.start()
    copy_in(0, 1).start()
    for at in range(1, 3):
        for g in range(groups):
            copy_in(at, g).start()
    barrier = pltpu.get_barrier_semaphore()
    far = [
        {"fsdp": other},
        {"ctx": (1 - z) * ring_len + q},
        {"ctx": (1 - z) * ring_len + q, "fsdp": other},
    ]
    for peer in far:
        pl.semaphore_signal(barrier, inc=1, device_id=peer, device_id_type=MESH)
    for hop in range(1, ring_len):
        pl.semaphore_signal(
            barrier,
            inc=1,
            device_id={"ctx": z * ring_len + lax.rem(q + hop, ring_len)},
            device_id_type=MESH,
        )

    for lead in leads:
        lead.wait()
    diagonal = lax.broadcasted_iota(jnp.int32, (heads, heads), 0) == lax.broadcasted_iota(
        jnp.int32, (heads, heads), 1
    )

    def column(ref):
        return jnp.sum(jnp.where(diagonal, ref[...], 0.0), axis=1, keepdims=True)

    rate = -jnp.exp(column(a_ref))
    bias = column(bias_ref)
    skip_line[...] = jnp.broadcast_to(column(skip_ref), skip_line.shape)
    step = softplus(dt_ref[...].astype(F32) + bias)
    row = lax.broadcasted_iota(jnp.int32, (tokens, tokens), 0)
    upto = row <= lax.broadcasted_iota(jnp.int32, (tokens, tokens), 1)
    running = dot_ones(step * rate, jnp.where(upto, 1.0, 0.0).astype(BF16))
    middle = 0.5 * running[:, tokens - 1 :]
    er = jnp.transpose(jnp.exp(running - middle))
    es = jnp.transpose(jnp.exp(middle - running) * step)
    ec = jnp.exp(middle)
    ec_ref[...] = jnp.broadcast_to(ec, ec_ref.shape)
    own_lane = lax.broadcasted_iota(jnp.int32, (heads, dim), 0) == lax.broadcasted_iota(
        jnp.int32, (heads, dim), 1
    )
    decay_row = jnp.sum(jnp.where(own_lane, ec * ec, 0.0), axis=0, keepdims=True)
    decay_rows[c] = jnp.broadcast_to(decay_row, decay_rows.shape[1:])

    def gain_copy():
        return pltpu.make_async_remote_copy(
            src_ref=gain_ref,
            dst_ref=gains.at[mine],
            send_sem=gain_send.at[0],
            recv_sem=gain_recv.at[0],
            device_id={"fsdp": other},
            device_id_type=MESH,
        )

    gains[mine] = gain_ref[...]

    halves[...] = b_ref[...].astype(F32)
    b_groups = [halves[pl.ds(g, tokens, stride=groups), :] for g in range(groups)]
    halves[...] = c_ref[...].astype(F32)
    c_groups = [halves[pl.ds(g, tokens, stride=groups), :] for g in range(groups)]
    for g in range(groups):
        b_one, c_one = b_groups[g].astype(BF16), c_groups[g].astype(BF16)
        b_turn = jnp.transpose(b_groups[g]).astype(BF16)
        c_turn = jnp.transpose(c_groups[g]).astype(BF16)
        bt[g] = wide([b_turn, b_turn])
        bb[g] = wide([b_one, b_one])
        cc[g] = wide([c_one, c_one])
        ctct[g] = wide([c_turn, c_turn])

    def remote(later, g, which, source, target, device):
        at = (int(later) * groups + g) * 9 + which
        return pltpu.make_async_remote_copy(
            src_ref=source,
            dst_ref=target,
            send_sem=send_sem.at[at],
            recv_sem=recv_sem.at[at],
            device_id={"ctx": device},
            device_id_type=MESH,
        )

    sibling = z * ring_len + y * CORES + (1 - c)

    def ring_device(hop):
        return z * ring_len + lax.rem(y + hop, RING) * CORES + c

    def sibling_decay():
        return pltpu.make_async_remote_copy(
            src_ref=decay_rows.at[c],
            dst_ref=decay_rows.at[c],
            send_sem=decay_send.at[0],
            recv_sem=decay_recv.at[0],
            device_id={"ctx": sibling},
            device_id_type=MESH,
        )

    def chip_decay(hop):
        return pltpu.make_async_remote_copy(
            src_ref=chip_rows.at[y],
            dst_ref=chip_rows.at[y],
            send_sem=decay_send.at[hop],
            recv_sem=decay_recv.at[hop],
            device_id={"ctx": ring_device(hop)},
            device_id_type=MESH,
        )

    def spread(row):
        return jnp.broadcast_to(
            jnp.sum(jnp.where(own_lane, row, 0.0), axis=1, keepdims=True), (heads, dim)
        )

    def core_decays():
        sibling_decay().wait()
        chip_rows[y] = decay_rows[0] * decay_rows[1]
        for hop in range(1, RING):
            chip_decay(hop).start()
        for core in range(CORES):
            decays[core] = spread(decay_rows[core, :1, :])

    def chip_decays():
        for hop in range(1, RING):
            chip_decay(hop).wait()
        for chip in range(RING):
            chains[chip] = spread(chip_rows[chip, :1, :])

    def first_swap(later, g):
        source = local if later else fresh
        return remote(
            later,
            g,
            0,
            source.at[pl.ds(g * per + (1 - c) * half, half)],
            sib.at[pl.ds(g * half, half)],
            sibling,
        )

    def scatter(later, g, hop):
        to = lax.rem(y + hop, RING)
        return remote(
            later,
            g,
            hop,
            pair.at[pl.ds(g * half + to * own, own)],
            scat.at[pl.ds(g * half + y * own, own)],
            ring_device(hop),
        )

    def cross_z(later, g):
        return remote(
            later,
            g,
            7,
            total.at[pl.ds(g * own, own)],
            ztotal.at[pl.ds(g * own, own)],
            (1 - z) * ring_len + q,
        )

    def give_back(later, g, hop):
        to = lax.rem(y + hop, RING)
        return remote(
            later,
            g,
            3 + hop,
            pref.at[pl.ds(g * half + to * own, own)],
            ret.at[pl.ds(g * half + y * own, own)],
            ring_device(hop),
        )

    def second_swap(later, g):
        target = behind if later else carried
        return remote(
            later,
            g,
            8,
            ret.at[pl.ds(g * half, half)],
            target.at[pl.ds(g * per + c * half, half)],
            sibling,
        )

    def combine(later, g):
        source = local if later else fresh
        second = 0 if later else 1
        first_swap(later, g).wait()

        def one(k):
            head = g * per + c * half + k
            decay = decays[second, pl.ds(head, 1), :]
            is_second = c == second
            mul_own = jnp.where(is_second, 1.0, decay)
            mul_sib = jnp.where(is_second, decay, 1.0)
            value = source[head] * mul_own + sib[g * half + k] * mul_sib
            pair[g * half + k] = value

        loop(half, one)
        for hop in range(1, RING):
            scatter(later, g, hop).start()
        for j in range(own):
            scat[g * half + y * own + j] = pair[g * half + y * own + j]

    def prefixes(later, g):
        for hop in range(1, RING):
            scatter(later, g, hop).wait()
        order = list(range(RING))[:: -1 if later else 1]
        for j in range(own):
            head = g * per + c * half + y * own + j
            state = jnp.zeros_like(scat[0])
            for chip in order:
                decay = chains[chip, pl.ds(head, 1), :]
                pref[g * half + chip * own + j] = state
                state = scat[g * half + chip * own + j] + decay * state
            total[g * own + j] = state

        @pl.when(z == (1 if later else 0))
        def _():
            cross_z(later, g).start()
            for hop in range(1, RING):
                give_back(later, g, hop).start()

    def second_chips(later, g):
        @pl.when(z == (0 if later else 1))
        def _():
            cross_z(later, g).wait_recv()
            order = list(range(RING))[:: -1 if later else 1]
            for j in range(own):
                head = g * per + c * half + y * own + j
                state = ztotal[g * own + j]
                for chip in order:
                    decay = chains[chip, pl.ds(head, 1), :]
                    pref[g * half + chip * own + j] += state
                    state = decay * state
            for hop in range(1, RING):
                give_back(later, g, hop).start()

    def returned(later, g):
        source = local if later else fresh
        target = behind if later else carried
        first = 1 if later else 0
        for j in range(own):
            ret[g * half + y * own + j] = pref[g * half + y * own + j]
        for hop in range(1, RING):
            give_back(later, g, hop).wait()

        @pl.when(z == (1 if later else 0))
        def _():
            cross_z(later, g).wait_send()

        def one(k):
            head = g * per + c * half + k
            decay = decays[first, pl.ds(head, 1), :]
            is_first = c == first
            before = ret[g * half + k]
            base = jnp.where(is_first, source[head], sib[g * half + k])
            after = base + decay * before
            target[head] = jnp.where(is_first, before, after)
            ret[g * half + k] = jnp.where(is_first, after, before)

        loop(half, one)
        second_swap(later, g).start()

    def states(g):
        temp = cots.at[g]
        temp[...] = x_in[:, g * per : (g + 1) * per, :].astype(F32).reshape(tokens * per, dim)
        for one in range(per):
            esb[g * per + one] = jnp.broadcast_to(
                es[:, g * per + one : g * per + one + 1], (tokens, dim)
            )

        def pair_at(hh):
            scaled = []
            for at in range(2):
                head = g * per + hh + at
                x_one = temp[pl.ds(hh + at, tokens, stride=per), :]
                xh[head] = x_one.astype(BF16)
                high, low = split(x_one * esb[head])
                xs_high[head] = high
                xs_low[head] = low
                scaled.append(tall([high, low]))
            state = dot(bt[g], wide(scaled))
            for at in range(2):
                head = g * per + hh + at
                fresh[head] = state[:, at * dim : (at + 1) * dim] * ec_ref[pl.ds(head, 1), :]

        loop(half // 2, lambda i: pair_at((1 - c) * half + 2 * i))
        if g == 0:
            pl.semaphore_wait(barrier, ring_len + 2)
            sibling_decay().start()
        first_swap(False, g).start()
        if g == 0:
            gain_copy().start()
        loop(half // 2, lambda i: pair_at(c * half + 2 * i))

    def scores(g):
        value = jnp.where(lower(tokens), dot(cc[g, :, :dim], bt[g, :, :tokens]), 0.0)
        high, low = split(value)
        causal_m[g] = wide([high, high, low])
        high, low = split(jnp.transpose(value))
        causal_t[g] = wide([high, high, low])

    def widen(g):
        temp = cots.at[g]
        temp[...] = gate_in[:, g * per : (g + 1) * per, :].astype(F32).reshape(tokens * per, dim)

        def one(hh):
            gate = temp[pl.ds(hh, tokens, stride=per), :]
            sig = sigmoid(gate)
            silu = gate * sig
            place = pl.ds(pl.multiple_of(hh * tokens, tokens), tokens)
            silus[g, place, :] = silu
            slopes[g, place, :] = sig + silu * (1.0 - sig)

        loop(per, one)
        keep = lax.broadcasted_iota(jnp.int32, (tokens, 1, 1), 0) < limit_ref[0]
        temp[...] = jnp.where(
            keep, out_in[:, g * per : (g + 1) * per, :].astype(F32), 0.0
        ).reshape(tokens * per, dim)

    def inside(g):
        for one in range(per):
            erb[g * per + one] = jnp.broadcast_to(
                er[:, g * per + one : g * per + one + 1], (tokens, dim)
            )

        def pair_at(i):
            hh = g * per + 2 * i
            right = wide(
                [tall([xs_high[hh + at], xs_low[hh + at], xs_high[hh + at]]) for at in range(2)]
            )
            scanned = dot(causal_m[g], right)
            for at in range(2):
                head = hh + at
                mixed[head] = scanned[:, at * dim : (at + 1) * dim] * erb[head] + xh[head].astype(
                    F32
                ) * skip_line[pl.ds(head, 1), :]

        loop(per // 2, pair_at)

    def gated_norm(g):
        square[...] = jnp.zeros_like(square)
        cross[...] = jnp.zeros_like(cross)

        def pair_at(hh):
            right = []
            for at in range(2):
                head = g * per + hh + at
                right.append(tall(split(carried[head] * ec_ref[pl.ds(head, 1), :])))
            scanned = dot(cc[g], wide(right))
            sum_square, sum_cross = square[...], cross[...]
            for at in range(2):
                head = g * per + hh + at
                mix = mixed[head] + scanned[:, at * dim : (at + 1) * dim] * erb[head]
                mixed[head] = mix
                place = pl.ds(pl.multiple_of((hh + at) * tokens, tokens), tokens)
                gated = mix * silus[g, place, :]
                cot = cots[g, pl.ds(hh + at, tokens, stride=per), :]
                upper = cot * gains[g, pl.ds(hh + at, 1), :]
                sum_square = sum_square + gated * gated
                sum_cross = sum_cross + upper * gated
            square[...] = sum_square
            cross[...] = sum_cross

        loop(half // 2, lambda i: pair_at(c * half + 2 * i))
        second_swap(False, g).wait()
        loop(half // 2, lambda i: pair_at((1 - c) * half + 2 * i))
        width = per * dim
        inverse = lax.rsqrt(jnp.sum(square[...], axis=1, keepdims=True) * (1.0 / width) + EPS)
        pull = inverse * inverse * inverse * (jnp.sum(cross[...], axis=1, keepdims=True) * (1.0 / width))
        square[...] = jnp.broadcast_to(inverse, square.shape)
        cross[...] = jnp.broadcast_to(pull, cross.shape)

    lane = lax.broadcasted_iota(jnp.int32, (tokens, per), 1)

    def put(ref, g, hh, values):
        ref[g] = jnp.where(lane == hh, values[0], jnp.where(lane == hh + 1, values[1], ref[g]))

    def pulled(g):
        rho_ref[g] = jnp.zeros((tokens, per), F32)

        def pair_at(hh):
            right, rhos = [], []
            for at in range(2):
                head = g * per + hh + at
                row = pl.ds(head, 1)
                place = pl.ds(pl.multiple_of((hh + at) * tokens, tokens), tokens)
                silu = silus[g, place, :]
                mix = mixed[head]
                gated = mix * silu
                natural = pl.ds(hh + at, tokens, stride=per)
                cot = cots[g, natural, :]
                inverse = square[...]
                ggain[row, :] = jnp.sum(cot * gated * inverse, axis=0, keepdims=True)
                grad_gated = inverse * (cot * gains[g, pl.ds(hh + at, 1), :]) - cross[...] * gated
                grad_mix = grad_gated * silu
                cots[g, natural, :] = grad_gated * mix * slopes[g, place, :]
                x_one = xh[head].astype(F32)
                skip = skip_line[row, :]
                gskip[row, :] = jnp.sum(grad_mix * x_one, axis=0, keepdims=True)
                rhos.append(jnp.sum(grad_mix * (mix - x_one * skip), axis=1, keepdims=True))
                mixed[head] = grad_mix * skip
                high, low = split(grad_mix * erb[head])
                y_high[head] = high
                y_low[head] = low
                right.append(tall([high, low]))
            put(rho_ref, g, hh, rhos)
            back = dot(ctct[g], wide(right))
            for at in range(2):
                head = g * per + hh + at
                local[head] = back[:, at * dim : (at + 1) * dim] * ec_ref[pl.ds(head, 1), :]

        loop(half // 2, lambda i: pair_at((1 - c) * half + 2 * i))
        first_swap(True, g).start()
        loop(half // 2, lambda i: pair_at(c * half + 2 * i))

    def gate_copy(g):
        place = pl.ds(g * per, per)
        return pltpu.make_async_copy(
            gate_in.at[:, place, :], ggate_hbm.at[:, place, :], out_sem.at[g]
        )

    def x_copy(g):
        place = pl.ds(g * per, per)
        return pltpu.make_async_copy(
            x_in.at[:, place, :], gx_hbm.at[:, place, :], out_sem.at[groups + g]
        )

    def inside_back(g, part):
        if part == 0:
            gate_in[:, g * per : (g + 1) * per, :] = (
                cots[g].reshape(tokens, per, dim).astype(BF16)
            )
            gate_copy(g).start()
            grad_m[...] = jnp.zeros_like(grad_m)
            grad_c[...] = jnp.zeros_like(grad_c)
            sigma_ref[g] = jnp.zeros((tokens, per), F32)

        def pair_at(i):
            hh = part * half + 2 * i
            sigmas = []
            head = g * per + hh
            yh = wide([y_high[head], y_high[head + 1]])
            yl = wide([y_low[head], y_low[head + 1]])
            x_high = wide([xs_high[head], xs_high[head + 1]])
            x_low = wide([xs_low[head], xs_low[head + 1]])
            left = wide([yh, yh, yl])
            grad_m[...] += dot_nt(left, wide([x_high, x_low, x_high]))
            s_high, s_low = split(
                wide(
                    [carried[head + at] * ec_ref[pl.ds(head + at, 1), :] for at in range(2)]
                )
            )
            grad_c[...] += dot_nt(left, wide([s_high, s_low, s_high]))
            grad_scaled = dot(causal_t[g], tall([yh, yl, yh]))
            for at in range(2):
                one = head + at
                inner = grad_scaled[:, at * dim : (at + 1) * dim] * esb[one]
                sigmas.append(jnp.sum(inner * xh[one].astype(F32), axis=1, keepdims=True))
                mixed[one] += inner
                decay = ec_ref[pl.ds(one, 1), :]
                fresh[one] += (decay * decay) * carried[one]
            put(sigma_ref, g, hh, sigmas)

        loop(half // 2, pair_at)
        if part == 0:
            return
        value = jnp.where(lower(tokens), grad_m[...], 0.0)
        high, low = split(value)
        part = grad_c[...] + dot(wide([high, low]), tall([bb[g, :, :dim], bb[g, :, :dim]]))
        halves[pl.ds(g, tokens, stride=groups), :] = part
        high, low = split(jnp.transpose(value))
        grad_b[g] = dot(wide([high, low]), tall([cc[g, :, :dim], cc[g, :, :dim]]))

    def last_sums(g):
        def pair_at(hh):
            head = g * per + hh
            parts, more = [], []
            for at in range(2):
                one = head + at
                decay = ec_ref[pl.ds(one, 1), :]
                rows[pl.ds(one, 1), :] = jnp.sum(behind[one] * fresh[one], axis=0, keepdims=True)
                parts.append(behind[one] * decay)
            grad_scaled = dot(bb[g], tall(split(wide(parts))))
            for at in range(2):
                one = head + at
                inner = grad_scaled[:, at * dim : (at + 1) * dim] * esb[one]
                more.append(jnp.sum(inner * xh[one].astype(F32), axis=1, keepdims=True))
                silus[g, pl.ds(hh + at, tokens, stride=per), :] = mixed[one] + inner
            sigma_ref[g] += jnp.where(lane == hh, more[0], jnp.where(lane == hh + 1, more[1], 0.0))

        loop(half // 2, lambda i: pair_at(c * half + 2 * i))
        second_swap(True, g).wait()
        loop(half // 2, lambda i: pair_at((1 - c) * half + 2 * i))
        here = slice(g * per, (g + 1) * per)
        sigma_t = jnp.transpose(sigma_ref[g])
        sums = dot_ones(
            jnp.transpose(rho_ref[g]) - sigma_t, jnp.where(lower(tokens), 1.0, 0.0).astype(BF16)
        )
        grad_log = sums + jnp.sum(rows[here, :], axis=1, keepdims=True)
        bias_here = column(bias_ref)[here]
        rate_here = -jnp.exp(column(a_ref)[here])
        value = dt_ref[here, :].astype(F32) + bias_here
        step_here = softplus(value)
        grad_dt = (sigma_t / step_here + grad_log * rate_here) * sigmoid(value)
        gdt_ref[here, :] = grad_dt.astype(BF16)
        return (
            jnp.sum(grad_log * step_here, axis=1, keepdims=True) * rate_here,
            jnp.sum(grad_dt, axis=1, keepdims=True),
            jnp.sum(gskip[here, :], axis=1, keepdims=True),
        )

    def last_x(g):
        x_in[:, g * per : (g + 1) * per, :] = silus[g].reshape(tokens, per, dim).astype(BF16)
        x_copy(g).start()

    def last_b(g):
        def pair_at(i):
            head = g * per + 2 * i
            s_high, s_low = split(
                wide([behind[head + at] * ec_ref[pl.ds(head + at, 1), :] for at in range(2)])
            )
            x_high = wide([xs_high[head], xs_high[head + 1]])
            x_low = wide([xs_low[head], xs_low[head + 1]])
            grad_b[g] += dot_nt(wide([x_high, x_high, x_low]), wide([s_high, s_low, s_high]))

        loop(per // 2, pair_at)

    def near_copy(ref, sems, hop):
        return pltpu.make_async_remote_copy(
            src_ref=ref.at[0],
            dst_ref=ref.at[hop],
            send_sem=sems[0].at[3 + hop],
            recv_sem=sems[1].at[3 + hop],
            device_id={"ctx": z * ring_len + lax.rem(q + hop, ring_len)},
            device_id_type=MESH,
        )

    def far_copy(source, target, sems, at):
        return pltpu.make_async_remote_copy(
            src_ref=source,
            dst_ref=target,
            send_sem=sems[0].at[1 + at],
            recv_sem=sems[1].at[1 + at],
            device_id=far[at],
            device_id_type=MESH,
        )

    gain_sems, small_sems = (gain_send, gain_recv), (small_send, small_recv)

    def gain_far(at):
        owner = mine if at == 1 else other
        return far_copy(
            ggain.at[pl.ds(pl.multiple_of(owner * per, per), per)], gain_swap.at[at], gain_sems, at
        )

    def small_far(at):
        return far_copy(small_all.at[0], small_swap.at[at], small_sems, at)

    copy_in(0, 0).wait()
    states(0)
    core_decays()
    combine(False, 0)
    copy_in(0, 1).wait()
    states(1)
    combine(False, 1)
    scores(0)
    inside(0)
    copy_in(1, 0).wait()
    copy_in(2, 0).wait()
    widen(0)
    chip_decays()
    prefixes(False, 0)
    scores(1)
    inside(1)
    second_chips(False, 0)
    copy_in(1, 1).wait()
    copy_in(2, 1).wait()
    widen(1)
    gain_copy().wait()
    prefixes(False, 1)
    second_chips(False, 1)
    returned(False, 0)
    gated_norm(0)
    pulled(0)
    combine(True, 0)
    returned(False, 1)
    gated_norm(1)
    pulled(1)
    combine(True, 1)
    prefixes(True, 0)
    inside_back(0, 0)
    second_chips(True, 0)
    for at in range(3):
        gain_far(at).start()
    inside_back(0, 1)
    prefixes(True, 1)
    inside_back(1, 0)
    second_chips(True, 1)
    for at in range(3):
        gain_far(at).wait()
    gain_all[0] = (
        gain_swap[0]
        + gain_swap[1]
        + gain_swap[2]
        + ggain[pl.ds(pl.multiple_of(mine * per, per), per), :]
    )
    for hop in range(1, ring_len):
        near_copy(gain_all, gain_sems, hop).start()
    returned(True, 0)
    inside_back(1, 1)
    sums = [last_sums(0)]
    last_x(0)
    returned(True, 1)
    sums.append(last_sums(1))
    tails[0].start()
    shifted = lax.broadcasted_iota(jnp.int32, (per, dim), 0) + per == lax.broadcasted_iota(
        jnp.int32, (per, dim), 1
    )
    small_all[0] = jnp.zeros(small_out.shape, F32)
    for at in range(3):
        small_all[0, at : at + 1, :] = jnp.sum(
            jnp.where(own_lane[:per], sums[0][at], 0.0) + jnp.where(shifted, sums[1][at], 0.0),
            axis=0,
            keepdims=True,
        )
    for at in range(3):
        small_far(at).start()
    last_x(1)
    last_b(0)
    for at in range(3):
        small_far(at).wait()
    small_all[0] += small_swap[0] + small_swap[1] + small_swap[2]
    for hop in range(1, ring_len):
        near_copy(small_all, small_sems, hop).start()
    last_b(1)
    gc_ref[...] = halves[...].astype(BF16)
    tails[2].start()
    for g in range(groups):
        halves[pl.ds(g, tokens, stride=groups), :] = grad_b[g]
    gb_ref[...] = halves[...].astype(BF16)
    tails[1].start()
    for hop in range(1, ring_len):
        near_copy(gain_all, gain_sems, hop).wait()
    gain_total = gain_all[0]
    for hop in range(1, ring_len):
        gain_total = gain_total + gain_all[hop]
    gain_out[...] = gain_total * scale
    tails[4].start()
    for hop in range(1, ring_len):
        near_copy(small_all, small_sems, hop).wait()
    small_total = small_all[0]
    for hop in range(1, ring_len):
        small_total = small_total + small_all[hop]
    small_out[...] = small_total * scale
    tails[3].start()
    for g in range(groups):
        gate_copy(g).wait()
        x_copy(g).wait()
    for tail in tails:
        tail.wait()


def store_kernel(gx_in, ggate_in, gdt_in, gb_in, gc_in, small_in, gain_in, *refs):
    outs = refs[:9]
    held, gdt, gb, gc, small, gain, lines, in_sems, out_sems = refs[9:]
    cuts = held.shape[0] // 2
    rows = gx_in.shape[0] // cuts
    jobs = []
    for at, (source, target) in enumerate(((gx_in, outs[0]), (ggate_in, outs[1]))):
        for cut in range(cuts):
            place = pl.ds(cut * rows, rows)
            jobs.append((source.at[place], held.at[at * cuts + cut], target.at[place]))
    jobs += [(gdt_in, gdt, outs[2]), (gb_in, gb, outs[3]), (gc_in, gc, outs[4])]
    jobs.append((gain_in, gain, outs[8]))
    count = len(jobs)
    into = [pltpu.make_async_copy(job[0], job[1], in_sems.at[at]) for at, job in enumerate(jobs)]
    away = [pltpu.make_async_copy(job[1], job[2], out_sems.at[at]) for at, job in enumerate(jobs)]
    lead = pltpu.make_async_copy(small_in, small, in_sems.at[count])
    lead.start()
    for copy in into:
        copy.start()
    lead.wait()
    for at in range(3):
        lines[at] = small[at : at + 1, : lines.shape[2]]
        away.append(
            pltpu.make_async_copy(lines.at[at], outs[5 + at], out_sems.at[count + at])
        )
        away[-1].start()
    for at in range(count):
        into[at].wait()
        away[at].start()
    for copy in away:
        copy.wait()


def per_device(
    x_input,
    gate_input,
    dt_raw,
    b_input,
    c_input,
    a_log,
    dt_bias,
    skip_weight,
    norm_gain,
    valid_len,
    grad_output,
):
    _, tokens, heads, dim = x_input.shape
    groups, state = b_input.shape[2:]
    per = heads // groups
    half = per // CORES
    own = half // RING
    count = lax.axis_size("ctx")
    ring_len = RING * CORES
    shape = jax.ShapeDtypeStruct
    anywhere = pl.BlockSpec(memory_space=pl.ANY)
    limit = valid_len - lax.axis_index("ctx") * tokens
    scale = 1.0 / math.sqrt(tokens * count * lax.axis_size("fsdp"))
    sems = pltpu.SemaphoreType.DMA

    def vmem(*dims, kind=F32):
        return pltpu.VMEM(dims, kind)

    scratch = [
        vmem(heads, tokens, kind=BF16),
        vmem(tokens * groups, state, kind=BF16),
        vmem(tokens * groups, state, kind=BF16),
        vmem(1, heads),
        vmem(1, heads),
        vmem(1, heads),
        vmem(per, dim),
        vmem(heads, tokens, kind=BF16),
        vmem(tokens * groups, state, kind=BF16),
        vmem(tokens * groups, state, kind=BF16),
        vmem(8, dim),
        vmem(per, dim),
        vmem(tokens, heads, dim, kind=BF16),
        vmem(tokens, heads, dim, kind=BF16),
        vmem(tokens, heads, dim, kind=BF16),
        vmem(heads, tokens, dim, kind=BF16),
        vmem(heads, tokens, dim, kind=BF16),
        vmem(heads, tokens, dim, kind=BF16),
        vmem(heads, tokens, dim),
        vmem(heads, tokens, dim),
        vmem(groups, tokens * per, dim),
        vmem(groups, tokens * per, dim),
        vmem(groups, tokens * per, dim),
        vmem(heads, tokens, dim),
        vmem(heads, tokens, dim, kind=BF16),
        vmem(heads, tokens, dim, kind=BF16),
        vmem(heads, state, dim),
        vmem(heads, state, dim),
        vmem(heads, state, dim),
        vmem(heads, state, dim),
        vmem(groups * half, state, dim),
        vmem(groups * half, state, dim),
        vmem(groups * half, state, dim),
        vmem(groups * half, state, dim),
        vmem(groups * half, state, dim),
        vmem(groups * own, state, dim),
        vmem(groups * own, state, dim),
        vmem(groups, tokens, 3 * tokens, kind=BF16),
        vmem(groups, tokens, 3 * tokens, kind=BF16),
        vmem(groups, state, 2 * tokens, kind=BF16),
        vmem(groups, tokens, 2 * state, kind=BF16),
        vmem(groups, tokens, 2 * state, kind=BF16),
        vmem(groups, state, 2 * tokens, kind=BF16),
        vmem(heads, dim),
        vmem(CORES, heads, dim),
        vmem(groups, per, dim),
        vmem(heads, dim),
        vmem(CORES, 8, dim),
        vmem(RING, 8, dim),
        vmem(RING, heads, dim),
        vmem(groups, tokens, per),
        vmem(groups, tokens, per),
        vmem(tokens, dim),
        vmem(tokens, dim),
        vmem(tokens, tokens),
        vmem(tokens, state),
        vmem(groups, tokens, state),
        vmem(tokens * groups, state),
        vmem(heads, dim),
        vmem(heads, dim),
        vmem(heads, dim),
        vmem(3, per, dim),
        vmem(ring_len, per, dim),
        vmem(3, 8, dim),
        vmem(ring_len, 8, dim),
        sems((3 * groups,)),
        sems((2 * groups,)),
        sems((7,)),
        sems((5,)),
        sems((ring_len,)),
        sems((ring_len,)),
        sems((2 * groups * 9,)),
        sems((2 * groups * 9,)),
        sems((3 + ring_len,)),
        sems((3 + ring_len,)),
        sems((3 + ring_len,)),
        sems((3 + ring_len,)),
    ]
    grad_x, ggate, grad_dt, grad_b, grad_c, small, gain = pl.pallas_call(
        functools.partial(mixer_kernel, scale, groups),
        in_specs=[pl.BlockSpec(memory_space=pltpu.SMEM), ] + [anywhere] * 10,
        out_specs=[anywhere] * 7,
        out_shape=[
            shape((tokens, heads, dim), BF16),
            shape((tokens, heads, dim), BF16),
            shape((heads, tokens), BF16),
            shape((tokens * groups, state), BF16),
            shape((tokens * groups, state), BF16),
            shape((8, dim), F32),
            shape((per, dim), F32),
        ],
        scratch_shapes=scratch,
        compiler_params=pltpu.CompilerParams(
            collective_id=0, has_side_effects=True, vmem_limit_bytes=VMEM_LIMIT
        ),
        name="mixer",
    )(
        limit,
        x_input[0],
        gate_input[0],
        grad_output[0],
        dt_raw[0],
        b_input.reshape(tokens * groups, state),
        c_input.reshape(tokens * groups, state),
        a_log.reshape(1, heads),
        dt_bias.reshape(1, heads),
        skip_weight.reshape(1, heads),
        norm_gain.reshape(per, dim),
    )
    made = (grad_x, ggate, grad_dt, grad_b, grad_c)
    line = shape((1, heads), F32)
    cuts = 4
    outs = pl.pallas_call(
        store_kernel,
        in_specs=[anywhere] * 7,
        out_specs=[anywhere] * 9,
        out_shape=[shape(a.shape, a.dtype) for a in made] + [line] * 3 + [shape((per, dim), F32)],
        scratch_shapes=[
            vmem(2 * cuts, tokens // cuts, heads, dim, kind=BF16),
            vmem(heads, tokens, kind=BF16),
            vmem(tokens * groups, state, kind=BF16),
            vmem(tokens * groups, state, kind=BF16),
            vmem(8, dim),
            vmem(per, dim),
            vmem(3, 1, heads),
            sems((2 * cuts + 5,)),
            sems((2 * cuts + 7,)),
        ],
        name="store",
    )(*made, small, gain)
    return (
        outs[0][None],
        outs[1][None],
        outs[2][None],
        outs[3].reshape(b_input.shape),
        outs[4].reshape(c_input.shape),
        outs[5].reshape(heads),
        outs[6].reshape(heads),
        outs[7].reshape(heads),
        outs[8].reshape(norm_gain.shape),
    )


def solution(mesh):
    placed = (
        P("fsdp", "ctx", "tp", None),
        P("fsdp", "ctx", "tp", None),
        P("fsdp", "tp", "ctx"),
        P("fsdp", "ctx", "tp", None),
        P("fsdp", "ctx", "tp", None),
        P("tp"),
        P("tp"),
        P("tp"),
        P(("tp", "fsdp")),
        P("fsdp"),
        P("fsdp", "ctx", "tp", None),
    )
    return jax.shard_map(
        per_device,
        mesh=mesh,
        in_specs=placed,
        out_specs=(
            P("fsdp", "ctx", "tp", None),
            P("fsdp", "ctx", "tp", None),
            P("fsdp", "tp", "ctx"),
            P("fsdp", "ctx", "tp", None),
            P("fsdp", "ctx", "tp", None),
            P("tp"),
            P("tp"),
            P("tp"),
            P(("tp", "fsdp")),
        ),
        check_vma=False,
    )
```
